512 devices in a mesh: sec: 2 (over x_lo), grp: 64 (over z, y), tp: 4 (over x_hi, core).
Axes of the slice: x: 4 (x_hi: 2, x_lo: 2; x = x_hi * 2 + x_lo), y: 8, z: 8, core: 2. Of those that a mesh axis runs over, the one named last changes fastest.
Arguments:
- latent_cache: bfloat16 [64, 2048, 576], P('grp', 'sec'), may hold values from -8 to 8
- new_latent: bfloat16 [3, 64, 576], P(None, 'grp'), may hold values from -6 to 6
- queries: bfloat16 [3, 64, 128, 576], P(None, 'grp', 'tp'), may hold values from -48 to 48
- lengths: int32 [64], P('grp'), may hold values from 1 to 2048, as said below
- token_rows: bfloat16 [3, 768, 3584], P(None, 'grp'), may hold values from -6 to 6
- routes: int32 [3, 768, 8], P(None, 'grp'), may hold values from 0 to 63, all different within a row; in each aligned block of 12 rows (0 to 11, 12 to 23, ..., all dimensions but the last counted through in order) at most 3 rows name the same one
- route_gates: float32 [3, 768, 8], P(None, 'grp'), may hold values from 0.1 to 1
- gate_proj: bfloat16 [64, 3584, 1024], P('grp', None, ('sec', 'tp')), may hold values from -0.09375 to 0.09375
- up_proj: bfloat16 [64, 3584, 1024], P('grp', None, ('sec', 'tp')), may hold values from -0.09375 to 0.09375
- down_proj: bfloat16 [64, 1024, 3584], P('grp', ('sec', 'tp')), may hold values from -0.1875 to 0.1875
Outputs:
- attention_out: bfloat16 [3, 64, 128, 512], P(None, 'grp', 'tp', 'sec')
- moe_out: bfloat16 [3, 768, 3584], P(None, 'grp', ('sec', 'tp'))
The draws below stay inside these ranges and needn't reach their ends.
Inputs may be any that keep to these rules, and one draw needn't show every extreme that they name: Request r attends to its first lengths[r] cached positions; some request uses all 2048. `routes`: each token names 8 different experts; within the 12 tokens of one index of grp at one step no expert is named more than 3 times, a bound that some block reaches.
All inputs are finite; a program needn't handle non-finite values.
Results may differ from the reference program's by a relative error of at most 0.0065.
Values may be sent and summed in bfloat16 or wider, within the bound.
No kernel may reach another device: no remote copies, remote signals or barrier semaphores. Data moves between devices by JAX's collectives and lax.ppermute only.
A program may use at most 128 MiB of HBM per device.

```python
import math
import jax
import jax.numpy as jnp
import numpy as np
from jax import lax

D = 3584
FE = 1024
EXPERTS = 64
TOPK = 8
CAP = 3
H = 128
KL = 512
STEPS = 3
TOK_DEV = 12
KC = 576
CTX = 2048
REQS = 64
TOKENS = 768
N_GRP = 64


def first_keys(key):
    normal_part = jax.random.normal(jax.random.fold_in(key, 101), (REQS, KC), jnp.float32)
    return normal_part


def draw_latent_cache(key, part):
    normal_part = first_keys(key)
    key = jax.random.fold_in(key, 1)
    field = jnp.clip(0.6 * jax.random.normal(key, (REQS, CTX, KC), jnp.float32), -3.6, 3.6)
    first_row = jnp.clip(0.6 * normal_part, -3.6, 3.6)
    field = field.at[:, 0, :].set(first_row)
    return field.astype(jnp.bfloat16)


def draw_queries(key, part):
    key = jax.random.fold_in(key, 2)
    field = jnp.clip(2.5 * jax.random.normal(key, (STEPS, REQS, H, KC), jnp.float32), -12.0, 12.0)
    return field.astype(jnp.bfloat16)


def draw_lengths(key, part):
    key = jax.random.fold_in(key, 3)
    counts = jax.random.randint(key, (REQS,), 1, CTX + 1)
    fullest = jax.random.randint(jax.random.fold_in(key, 4), (), 0, REQS)
    return counts.at[fullest].set(CTX).astype(jnp.int32)


def steps_of(stream_key, extent, split, low, largest):
    def one(position, blocks):
        draws = jax.random.uniform(jax.random.fold_in(jax.random.fold_in(stream_key, 6), position), (blocks,), jnp.float32, low / len(split), largest / len(split))
        return jnp.repeat(jnp.exp(draws), extent[position] // blocks).reshape((-1,) + (1,) * (len(extent) - position - 1))

    loudness = one(*split[0])
    for cut in split[1:]:
        loudness = loudness * one(*cut)
    return loudness


def deal_out(stream_key, own, number, rows, number_of, top, bound, lean):
    ranking = jax.random.permutation(stream_key, number_of)
    packed, ordinary = load_shares(number_of, rows * top, bound, lean, True), load_shares(number_of, rows * top, bound, lean, False)
    places = jnp.arange(number_of)

    def named(sizes, rotation):
        used = int((sizes > 0).sum())
        fixed = max(1, used // 4)
        shifted = fixed + (places - fixed + rotation * (used - fixed)) % max(1, number_of - fixed)
        return jnp.zeros((number_of,), jnp.int32).at[ranking[jnp.where(places < fixed, places, shifted)]].set(jnp.asarray(sizes, jnp.int32))

    sizes = jnp.where(number % 4 == 0, named(packed, number // 4), named(ordinary, number - number // 4 - 1))
    mixed = jax.random.permutation(jax.random.fold_in(own, 3), number_of)
    donor, receiver = mixed[0:number_of // 2 * 2:2], mixed[1:number_of // 2 * 2:2]
    room = jnp.minimum(sizes[donor] - 1, bound - sizes[receiver]) // 2
    room = jnp.where((donor == ranking[0]) | (receiver == ranking[0]) | (sizes[receiver] == 0), 0, jnp.maximum(room, 0))
    shifted = jax.random.randint(jax.random.fold_in(own, 4), (number_of // 2,), 0, 1 << 20) % (room + 1)
    sizes = sizes.at[donor].add(-shifted).at[receiver].add(shifted)
    members = jnp.searchsorted(jnp.cumsum(sizes), jnp.arange(rows * top), side="right").astype(jnp.int32)
    listing = members.reshape(top, rows).T
    listing = listing[jax.random.permutation(jax.random.fold_in(own, 1), rows)]
    rotation = jax.random.randint(jax.random.fold_in(own, 2), (rows, 1), 0, top)
    return jnp.take_along_axis(listing, (jnp.arange(top)[None, :] + rotation) % top, axis=1)


def load_shares(number_of, total, limit, skew, full):
    loads = [(1 << 20) // math.isqrt(rank ** skew) + 1 for rank in range(1, number_of + 1)]
    largest = limit if full else min(limit, max(-(-total // number_of), total * loads[0] // sum(loads)))
    least = 1 if total - largest >= number_of - 1 else 0
    given, surplus = [largest] + [least] * (number_of - 1), total - largest - least * (number_of - 1)
    while surplus > 0:
        movable = [i for i in range(1, number_of) if given[i] < largest] or [i for i in range(1, number_of) if given[i] < limit]
        mass, remaining = sum([loads[i] for i in movable]), surplus
        for i in movable:
            extra = min(limit - given[i], max(1, remaining * loads[i] // mass), surplus)
            given[i] = given[i] + extra
            surplus = surplus - extra
    return np.array(given)


def gaussian(own_key, shape, spread, bound, cuts=(), kind=jnp.bfloat16):
    entries = spread * jax.random.normal(own_key, shape, jnp.float32)
    if cuts:
        entries = entries * steps_of(own_key, shape, cuts, -0.22, 0.18)
    return jnp.clip(entries, -bound, bound).astype(kind)


def setup_inputs(seed: int = 0) -> dict:
    streams_of = jax.random.split(jax.random.key(seed), 11)
    latent_cache = draw_latent_cache(jax.random.fold_in(streams_of[10], 71), 0)
    new_latent = gaussian(streams_of[1], (STEPS, REQS, KC), 1.0, 6.0, ((1, 64),))
    queries = draw_queries(jax.random.fold_in(streams_of[10], 71), 0)
    lengths = draw_lengths(jax.random.fold_in(streams_of[10], 71), 0)
    token_rows = gaussian(streams_of[4], (STEPS, TOKENS, D), 1.0, 6.0, ((1, 64),))
    routes_keys = jax.random.split(jax.random.fold_in(streams_of[5], 1), STEPS * TOKENS // TOK_DEV)
    routes_turns = jax.random.permutation(jax.random.fold_in(streams_of[5], 3), STEPS * TOKENS // TOK_DEV)
    routes = jax.vmap(lambda own, number: deal_out(jax.random.fold_in(streams_of[5], 2), own, number, TOK_DEV, EXPERTS, TOPK, CAP, 2))(routes_keys, routes_turns).reshape((STEPS, TOKENS, TOPK))
    route_gates = jnp.clip(jnp.exp(math.log(1.0) - 2.3025851 * jax.random.uniform(streams_of[6], (STEPS, TOKENS, TOPK), jnp.float32) ** steps_of(streams_of[6], (STEPS, TOKENS, TOPK), ((1, 64),), -0.2, 0.2)), 0.1, 1.0)
    gate_proj = gaussian(streams_of[7], (EXPERTS, D, FE), D ** -0.5, 0.09375, ((0, 64), (2, 8)))
    up_proj = gaussian(streams_of[8], (EXPERTS, D, FE), D ** -0.5, 0.09375, ((0, 64), (2, 8)))
    down_proj = gaussian(streams_of[9], (EXPERTS, FE, D), FE ** -0.5, 0.1875, ((0, 64), (1, 8)))
    return {"latent_cache": latent_cache, "new_latent": new_latent, "queries": queries, "lengths": lengths, "token_rows": token_rows, "routes": routes, "route_gates": route_gates, "gate_proj": gate_proj, "up_proj": up_proj, "down_proj": down_proj}


score_scale = 192.0 ** -0.5


def attend_request(args):
    cache_rows, new_rows, query_rows, length = args
    cache_wide = cache_rows.astype(jnp.float32)
    new_wide = new_rows.astype(jnp.float32)
    query_wide = query_rows.astype(jnp.float32)
    cached_scores = jnp.einsum('shk,ck->shc', query_wide, cache_wide, precision=lax.Precision.HIGHEST) * score_scale
    new_scores = jnp.einsum('shk,tk->sht', query_wide, new_wide, precision=lax.Precision.HIGHEST) * score_scale
    usable = (jnp.arange(cache_rows.shape[0], dtype=jnp.int32) < length)[None, None, :]
    step_ids = jnp.arange(new_rows.shape[0], dtype=jnp.int32)
    causal = (step_ids[:, None] >= step_ids[None, :])[:, None, :]
    top_score = jnp.maximum(jnp.max(jnp.where(usable, cached_scores, -jnp.inf), axis=-1),
                            jnp.max(jnp.where(causal, new_scores, -jnp.inf), axis=-1))
    cached_exp = jnp.where(usable, jnp.exp(cached_scores - top_score[..., None]), 0.0)
    new_exp = jnp.where(causal, jnp.exp(new_scores - top_score[..., None]), 0.0)
    weight_sum = jnp.sum(cached_exp, axis=-1) + jnp.sum(new_exp, axis=-1)
    cached_weights = lax.optimization_barrier(cached_exp.astype(jnp.bfloat16)).astype(jnp.float32)
    context = jnp.einsum('shc,cv->shv', cached_weights, cache_wide[:, :KL], precision=lax.Precision.HIGHEST)
    context = context + jnp.einsum('sht,tv->shv', new_exp, new_wide[:, :KL], precision=lax.Precision.HIGHEST)
    return (context / weight_sum[..., None]).astype(jnp.bfloat16)


def run_expert(args):
    expert_rows, gate_matrix, up_matrix, down_matrix = args
    gate_pre = jnp.dot(expert_rows, gate_matrix, preferred_element_type=jnp.float32)
    up_pre = jnp.dot(expert_rows, up_matrix, preferred_element_type=jnp.float32)
    hidden = (jax.nn.silu(gate_pre) * up_pre).astype(jnp.bfloat16)
    return jnp.dot(hidden, down_matrix, preferred_element_type=jnp.float32)


def reference(latent_cache, new_latent, queries, lengths, token_rows, routes, route_gates, gate_proj, up_proj, down_proj):
    attention_out = lax.map(attend_request, (latent_cache, jnp.transpose(new_latent, (1, 0, 2)),
                                             jnp.transpose(queries, (1, 0, 2, 3)), lengths))
    attention_out = jnp.transpose(attention_out, (1, 0, 2, 3))
    pair_count = TOK_DEV * TOPK
    results = []
    for step in range(STEPS):
        block_ids = routes[step].reshape(N_GRP, pair_count)
        onehot = (block_ids[:, :, None] == jnp.arange(EXPERTS, dtype=jnp.int32)[None, None, :]).astype(jnp.int32)
        before = jnp.cumsum(onehot, axis=1) - onehot
        slot_ids = jnp.sum(onehot * before, axis=2)
        places = (jnp.arange(N_GRP, dtype=jnp.int32)[:, None] * CAP + slot_ids).reshape(-1).astype(jnp.int32)
        experts_flat = block_ids.reshape(-1).astype(jnp.int32)
        copies = jnp.repeat(token_rows[step], TOPK, axis=0)
        buffers = jnp.zeros((EXPERTS, N_GRP * CAP, D), jnp.bfloat16).at[experts_flat, places].set(copies)
        expert_out = lax.map(run_expert, (buffers, gate_proj, up_proj, down_proj))
        picked = expert_out[experts_flat, places].reshape(TOKENS, TOPK, D)
        combined = jnp.sum(picked * route_gates[step][:, :, None], axis=1)
        results.append(combined.astype(jnp.bfloat16))
    return attention_out, jnp.stack(results)
```

```python
import jax
import jax.numpy as jnp
from jax import lax
from jax.experimental import pallas as pl
from jax.experimental.pallas import tpu as pltpu
from jax.sharding import PartitionSpec as P

CAP = 3
KL = 512
ROWS = 8
HALF = 64

score_scale = 192.0 ** (-0.5)
neg_big = -1e30
BF = jnp.bfloat16
F32 = jnp.float32
LINE = ("sec", "tp")

SMEM = pl.BlockSpec(memory_space=pltpu.SMEM)
VMEM = pl.BlockSpec(memory_space=pltpu.VMEM)


def dot(a, b, dims=((1,), (0,))):
    return lax.dot_general(a, b, (dims, ((), ())), preferred_element_type=F32)


def iota(shape, axis):
    return lax.broadcasted_iota(jnp.int32, shape, axis)


def call(body, out_shape, in_specs, flops, moved, name):
    single = not isinstance(out_shape, (list, tuple))
    return pl.pallas_call(
        body,
        out_shape=out_shape,
        in_specs=in_specs,
        out_specs=VMEM if single else [VMEM] * len(out_shape),
        compiler_params=pltpu.CompilerParams(vmem_limit_bytes=40 * 1024 * 1024),
        cost_estimate=pl.CostEstimate(flops=flops, bytes_accessed=moved, transcendentals=0),
        name=name,
    )


def attend_body(info, q_ref, cache_ref, new_ref, send_ref, keep_ref):
    section, length = info[0], info[1]
    q = q_ref[...]
    rows, local_length = q.shape[0], cache_ref.shape[0]
    steps = new_ref.shape[0]
    heads = rows // steps
    scores = dot(q, cache_ref[...], ((1,), (1,))) * score_scale
    usable = iota((rows, local_length), 1) + section * local_length < length
    scores = jnp.where(usable, scores, neg_big)
    top = jnp.max(scores, axis=1, keepdims=True)
    new_rows = new_ref[...]
    fresh = dot(q, new_rows, ((1,), (1,))) * score_scale
    step_of = iota((rows, steps), 0) // heads
    causal = (iota((rows, steps), 1) <= step_of) & (section == 0)
    fresh = jnp.where(causal, fresh, neg_big)
    top = jnp.maximum(top, jnp.max(fresh, axis=1, keepdims=True))
    weights = jnp.where(usable, jnp.exp(scores - top), 0.0)
    new_weights = jnp.where(causal, jnp.exp(fresh - top), 0.0)
    total = jnp.sum(weights, axis=1, keepdims=True) + jnp.sum(new_weights, axis=1, keepdims=True)
    out = dot(weights.astype(BF), cache_ref[:, :KL])
    values = new_rows[:, :KL].astype(F32)
    for t in range(steps):
        out = out + new_weights[:, t : t + 1] * values[t : t + 1, :]
    mine = section == 0
    half = KL // 2
    keep_ref[:, :half] = jnp.where(mine, out[:, :half], out[:, half:])
    send_ref[:, :half] = jnp.where(mine, out[:, half:], out[:, :half])
    for ref in (keep_ref, send_ref):
        ref[:, half : half + 128] = jnp.broadcast_to(top, (rows, 128))
        ref[:, half + 128 : half + 256] = jnp.broadcast_to(total, (rows, 128))


def merge_body(one_ref, two_ref, out_ref):
    half = out_ref.shape[1]
    top_one, top_two = one_ref[:, half : half + 1], two_ref[:, half : half + 1]
    top = jnp.maximum(top_one, top_two)
    factor_one, factor_two = jnp.exp(top_one - top), jnp.exp(top_two - top)
    total = (
        one_ref[:, half + 128 : half + 129] * factor_one
        + two_ref[:, half + 128 : half + 129] * factor_two
    )
    out = one_ref[:, :half] * factor_one + two_ref[:, :half] * factor_two
    out_ref[...] = (out / total).astype(BF)


def named_slots(routes, experts):
    tokens, picks = routes.shape
    experts_of = iota((tokens, experts), 1)
    named = jnp.zeros((tokens, experts), F32)
    for k in range(picks):
        named = named + (routes[:, k : k + 1] == experts_of).astype(F32)
    earlier = (iota((tokens, tokens), 1) < iota((tokens, tokens), 0)).astype(BF)
    before = dot(earlier, named.astype(BF))
    return jnp.where(named > 0.5, before, -1.0)


def spread(values, experts):
    rows = experts * ROWS
    repeat = (iota((experts, rows), 1) // ROWS == iota((experts, rows), 0)).astype(BF)
    return dot(values.astype(BF), repeat)


def pack_body(where_ref, tokens_ref, routes_ref, out_ref):
    chip, core = where_ref[0], where_ref[1]
    rows = out_ref.shape[0]
    experts = rows // ROWS
    steps, tokens = routes_ref.shape[0], routes_ref.shape[1]
    part = tokens_ref.shape[2] // 8
    place = iota((tokens, rows), 1) % ROWS
    main = jnp.zeros((rows, part), F32)
    for step in range(steps):
        columns = tokens_ref[step, :, pl.ds(pl.multiple_of(chip * 2 * part, 128), 2 * part)]
        own = jnp.where(core == 0, columns[:, :part], columns[:, part:])
        slots = spread(named_slots(routes_ref[step], experts), experts)
        wanted = (place - CAP * step).astype(F32)
        chosen = ((slots == wanted) & (wanted >= 0)).astype(BF)
        main = main + dot(chosen, own, ((0,), (0,)))
        if step == steps - 1:
            last = dot((slots == CAP - 1.0).astype(BF), own, ((0,), (0,)))
    out_ref[:, :part] = main.astype(BF)
    row = iota((rows, HALF), 0) % ROWS
    tail = jnp.zeros((rows, HALF), F32)
    for i in range(part // HALF):
        tail = tail + jnp.where(row == i, last[:, i * HALF : (i + 1) * HALF], 0.0)
    out_ref[:, part:] = tail.astype(BF)


def gates_body(routes_ref, gates_ref, out_ref):
    steps, tokens, picks = routes_ref.shape
    rows = out_ref.shape[2]
    experts = rows // ROWS
    out_ref[...] = jnp.zeros(out_ref.shape, BF)
    place = iota((tokens, rows), 1) % ROWS
    experts_of = iota((tokens, experts), 1)
    for step in range(steps):
        routes = routes_ref[step]
        gates = gates_ref[step]
        slots = spread(named_slots(routes, experts), experts)
        gate = jnp.zeros((tokens, experts), F32)
        for k in range(picks):
            gate = gate + jnp.where(routes[:, k : k + 1] == experts_of, gates[:, k : k + 1], 0.0)
        high = gate.astype(BF)
        low = gate - high.astype(F32)
        wanted = (place - CAP * step).astype(F32)
        chosen = (slots == wanted) & (wanted >= 0)
        for n, part in enumerate((spread(high, experts), spread(low, experts))):
            out_ref[n, 16 * step : 16 * step + tokens, :] = jnp.where(chosen, part, 0.0).astype(BF)
            if step == steps - 1:
                for i in range(7):
                    start = 16 * (steps + i)
                    out_ref[n, start : start + tokens, :] = jnp.where(
                        (slots == CAP - 1.0) & (place == i), part, 0.0
                    ).astype(BF)


def hidden_body(info, *refs):
    pieces, (gate_ref, up_ref, out_ref) = refs[:8], refs[8:]
    rows = pieces[0].shape[0]
    experts = rows // ROWS
    part = gate_ref.shape[0] // 8
    me = info[0]

    def weights(k, start, size):
        offset = pl.multiple_of((me ^ k) * part + start, HALF)
        return jnp.concatenate(
            [gate_ref[pl.ds(offset, size), :], up_ref[pl.ds(offset, size), :]], axis=1
        )

    def finish(pre):
        wide = pre.shape[1] // 2
        gate, up = pre[:, :wide], pre[:, wide:]
        return (gate / (1.0 + jnp.exp(-gate)) * up).astype(BF)

    pre = jnp.zeros((rows, 2 * out_ref.shape[1]), F32)
    for k in range(8):
        pre = pre + dot(pieces[k][:, :part], weights(k, 0, part))
    out_ref[:rows, :] = finish(pre)
    tail = jnp.concatenate([pieces[k][:, part:] for k in range(8)], axis=1)
    count = part // HALF
    source = iota((count * experts, rows), 0)
    wanted = (source % experts) * ROWS + source // experts
    chosen = (iota((count * experts, rows), 1) == wanted).astype(BF)
    ninth = dot(chosen, tail).astype(BF)
    pre = jnp.zeros((experts, 2 * out_ref.shape[1]), F32)
    for i in range(count):
        part_weights = jnp.concatenate([weights(k, i * HALF, HALF) for k in range(8)], axis=0)
        pre = pre + dot(ninth[i * experts : (i + 1) * experts], part_weights)
    out_ref[rows:, :] = finish(pre)


def down_body(*refs):
    hidden, down, out_ref = refs[:8], refs[8:16], refs[16]
    rows, part = out_ref.shape[0], down[0].shape[1]
    experts = rows // ROWS
    total = jnp.zeros((hidden[0].shape[0], part), F32)
    for k in range(8):
        total = total + dot(hidden[k][...], down[k][...])
    total = total.astype(BF)
    out_ref[:, :part] = total[:rows]
    repeat = (iota((rows, experts), 0) // ROWS == iota((rows, experts), 1)).astype(BF)
    last = dot(repeat, total[rows:])
    row = iota((rows, HALF), 0) % ROWS
    tail = jnp.zeros((rows, HALF), F32)
    for i in range(part // HALF):
        tail = tail + jnp.where(row == i, last[:, i * HALF : (i + 1) * HALF], 0.0)
    out_ref[:, part:] = tail.astype(BF)


def slices_body(info, down_ref, *outs):
    me = info[0]
    part = outs[0].shape[1]
    for k in range(8):
        other = me ^ k
        columns = down_ref[:, pl.ds(pl.multiple_of((other // 2) * 2 * part, 128), 2 * part)]
        outs[k][...] = jnp.where(other % 2 == 0, columns[:, :part], columns[:, part:])


def combine_body(gates_ref, rows_ref, out_ref):
    steps, tokens, part = out_ref.shape
    values = rows_ref[...]
    total = dot(gates_ref[0], values) + dot(gates_ref[1], values)
    for step in range(steps):
        out = total[16 * step : 16 * step + tokens, :part]
        if step == steps - 1:
            more = [
                total[16 * (steps + i) : 16 * (steps + i) + tokens, part:]
                for i in range(part // HALF)
            ]
            out = out + jnp.concatenate(more, axis=1)
        out_ref[step] = out.astype(BF)


def swap(value, k):
    return lax.ppermute(value, LINE, [(d, d ^ k) for d in range(8)])


def gather_line(own):
    middle = own.shape[0] // 2 // 16 * 16
    pieces = [own] + [None] * 7
    pieces[4] = swap(own, 4)
    pieces[6] = swap(own, 6)
    pieces[1] = swap(own, 1)
    first = swap(pieces[4][:middle], 6)
    second = swap(pieces[6][middle:], 4)
    pieces[5] = swap(pieces[4], 1)
    pieces[7] = swap(pieces[6], 1)
    pieces[2] = jnp.concatenate([first, second], axis=0)
    pieces[3] = jnp.concatenate([swap(first, 1), swap(second, 1)], axis=0)
    return pieces


def local(
    latent_cache,
    new_latent,
    queries,
    lengths,
    token_rows,
    routes,
    route_gates,
    gate_proj,
    up_proj,
    down_proj,
):
    section = lax.axis_index("sec")
    me = lax.axis_index(LINE)
    experts = lax.axis_size("grp")
    rows = experts * ROWS
    steps, tokens, width = token_rows.shape
    part = width // 8
    units = gate_proj.shape[2]
    here = me.astype(jnp.int32).reshape(1)

    packed = call(
        pack_body, jax.ShapeDtypeStruct((rows, part + HALF), BF), [SMEM, VMEM, VMEM],
        10**8, 10**6, "pack",
    )(jnp.stack([me // 2, me % 2]).astype(jnp.int32), token_rows, routes)
    arrived = lax.all_to_all(
        packed.reshape(experts, ROWS, part + HALF), "grp", split_axis=0, concat_axis=0, tiled=True
    ).reshape(rows, part + HALF)

    down = call(
        slices_body, [jax.ShapeDtypeStruct((units, part), BF)] * 8, [SMEM, VMEM],
        10**6, 2 * 10**6, "slices",
    )(here, down_proj.reshape(units, width))
    down = [down[0]] + [swap(down[k], k) for k in range(1, 8)]

    gates = call(
        gates_body,
        jax.ShapeDtypeStruct((2, 16 * (steps + part // HALF), rows), BF),
        [VMEM, VMEM], 10**8, 10**6, "gates",
    )(routes, route_gates)

    heads = queries.shape[2]
    send, keep = call(
        attend_body, [jax.ShapeDtypeStruct((steps * heads, KL // 2 + 256), F32)] * 2,
        [SMEM, VMEM, VMEM, VMEM], 3 * 10**8, 2 * 10**6, "attend",
    )(
        jnp.stack([section.astype(jnp.int32), lengths[0]]),
        queries.reshape(steps * heads, queries.shape[3]),
        latent_cache.reshape(latent_cache.shape[1:]),
        new_latent.reshape(steps, new_latent.shape[2]),
    )
    other = swap(send, 4)
    attention = call(
        merge_body, jax.ShapeDtypeStruct((steps * heads, KL // 2), BF), [VMEM, VMEM],
        10**6, 10**6, "merge",
    )(keep, other)

    pieces = gather_line(arrived)
    hidden = call(
        hidden_body, jax.ShapeDtypeStruct((rows + experts, units), BF), [SMEM] + [VMEM] * 10,
        10**9, 6 * 10**6, "hidden",
    )(here, *pieces, gate_proj.reshape(width, units), up_proj.reshape(width, units))
    hidden = gather_line(hidden)
    outgoing = call(
        down_body, jax.ShapeDtypeStruct((rows, part + HALF), BF), [VMEM] * 16,
        10**9, 3 * 10**6, "down",
    )(*hidden, *down)
    returned = lax.all_to_all(
        outgoing.reshape(experts, ROWS, part + HALF), "grp", split_axis=0, concat_axis=0, tiled=True
    ).reshape(rows, part + HALF)
    moe = call(
        combine_body, jax.ShapeDtypeStruct((steps, tokens, part), BF), [VMEM, VMEM],
        10**8, 10**6, "combine",
    )(gates, returned)
    return attention.reshape(steps, 1, heads, KL // 2), moe


def solution(mesh):
    in_specs = (
        P("grp", "sec", None),
        P(None, "grp", None),
        P(None, "grp", "tp", None),
        P("grp"),
        P(None, "grp", None),
        P(None, "grp", None),
        P(None, "grp", None),
        P("grp", None, ("sec", "tp")),
        P("grp", None, ("sec", "tp")),
        P("grp", ("sec", "tp"), None),
    )
    out_specs = (P(None, "grp", "tp", "sec"), P(None, "grp", ("sec", "tp")))
    return jax.shard_map(local, mesh=mesh, in_specs=in_specs, out_specs=out_specs, check_vma=False)
```

```python
import jax
import jax.numpy as jnp
from jax import lax
from jax.experimental import pallas as pl
from jax.experimental.pallas import tpu as pltpu
from jax.sharding import PartitionSpec as P

CAP = 3
KL = 512
ROWS = 8
HALF = 64

score_scale = 192.0 ** (-0.5)
neg_big = -1e30
BF = jnp.bfloat16
F32 = jnp.float32
LINE = ("sec", "tp")

SMEM = pl.BlockSpec(memory_space=pltpu.SMEM)
VMEM = pl.BlockSpec(memory_space=pltpu.VMEM)
ANY = pl.BlockSpec(memory_space=pl.ANY)


def dot(a, b, dims=((1,), (0,))):
    return lax.dot_general(a, b, (dims, ((), ())), preferred_element_type=F32)


def iota(shape, axis):
    return lax.broadcasted_iota(jnp.int32, shape, axis)


def call(body, out_shape, in_specs, flops, moved, name):
    single = not isinstance(out_shape, (list, tuple))
    return pl.pallas_call(
        body,
        out_shape=out_shape,
        in_specs=in_specs,
        out_specs=VMEM if single else [VMEM] * len(out_shape),
        compiler_params=pltpu.CompilerParams(vmem_limit_bytes=40 * 1024 * 1024),
        cost_estimate=pl.CostEstimate(flops=flops, bytes_accessed=moved, transcendentals=0),
        name=name,
    )


def attend_body(info, q_ref, cache_ref, new_ref, send_ref, keep_ref):
    section, length = info[0], info[1]
    q = q_ref[...]
    rows, local_length = q.shape[0], cache_ref.shape[0]
    steps = new_ref.shape[0]
    heads = rows // steps
    scores = dot(q, cache_ref[...], ((1,), (1,))) * score_scale
    usable = iota((rows, local_length), 1) + section * local_length < length
    scores = jnp.where(usable, scores, neg_big)
    top = jnp.max(scores, axis=1, keepdims=True)
    new_rows = new_ref[...]
    fresh = dot(q, new_rows, ((1,), (1,))) * score_scale
    step_of = iota((rows, steps), 0) // heads
    causal = (iota((rows, steps), 1) <= step_of) & (section == 0)
    fresh = jnp.where(causal, fresh, neg_big)
    top = jnp.maximum(top, jnp.max(fresh, axis=1, keepdims=True))
    weights = jnp.where(usable, jnp.exp(scores - top), 0.0)
    new_weights = jnp.where(causal, jnp.exp(fresh - top), 0.0)
    total = jnp.sum(weights, axis=1, keepdims=True) + jnp.sum(new_weights, axis=1, keepdims=True)
    out = dot(weights.astype(BF), cache_ref[:, :KL])
    values = new_rows[:, :KL].astype(F32)
    for t in range(steps):
        out = out + new_weights[:, t : t + 1] * values[t : t + 1, :]
    mine = section == 0
    half = KL // 2
    keep_ref[:, :half] = jnp.where(mine, out[:, :half], out[:, half:])
    send_ref[:, :half] = jnp.where(mine, out[:, half:], out[:, :half])
    for ref in (keep_ref, send_ref):
        ref[:, half : half + 128] = jnp.broadcast_to(top, (rows, 128))
        ref[:, half + 128 : half + 256] = jnp.broadcast_to(total, (rows, 128))


def merge_body(one_ref, two_ref, out_ref):
    half = out_ref.shape[1]
    top_one, top_two = one_ref[:, half : half + 1], two_ref[:, half : half + 1]
    top = jnp.maximum(top_one, top_two)
    factor_one, factor_two = jnp.exp(top_one - top), jnp.exp(top_two - top)
    total = (
        one_ref[:, half + 128 : half + 129] * factor_one
        + two_ref[:, half + 128 : half + 129] * factor_two
    )
    out = one_ref[:, :half] * factor_one + two_ref[:, :half] * factor_two
    out_ref[...] = (out / total).astype(BF)


def named_slots(routes, experts):
    tokens, picks = routes.shape
    experts_of = iota((tokens, experts), 1)
    named = jnp.zeros((tokens, experts), F32)
    for k in range(picks):
        named = named + (routes[:, k : k + 1] == experts_of).astype(F32)
    earlier = (iota((tokens, tokens), 1) < iota((tokens, tokens), 0)).astype(BF)
    before = dot(earlier, named.astype(BF))
    return jnp.where(named > 0.5, before, -1.0)


def spread(values, experts):
    rows = experts * ROWS
    repeat = (iota((experts, rows), 1) // ROWS == iota((experts, rows), 0)).astype(BF)
    return dot(values.astype(BF), repeat)


def pack_body(where_ref, tokens_ref, routes_ref, out_ref, tokens_here, routes_here, sems):
    chip, core = where_ref[0], where_ref[1]
    rows = out_ref.shape[0]
    experts = rows // ROWS
    steps, tokens = routes_ref.shape[0], routes_ref.shape[1]
    part = tokens_ref.shape[2] // 8
    columns = pl.ds(pl.multiple_of(chip * 2 * part, 128), 2 * part)
    fetch_routes = pltpu.make_async_copy(routes_ref, routes_here, sems.at[0])
    fetch_tokens = pltpu.make_async_copy(tokens_ref.at[:, :, columns], tokens_here, sems.at[1])
    fetch_routes.start()
    fetch_tokens.start()
    place = iota((tokens, rows), 1) % ROWS
    fetch_routes.wait()
    slots = [spread(named_slots(routes_here[step], experts), experts) for step in range(steps)]
    fetch_tokens.wait()
    main = jnp.zeros((rows, part), F32)
    for step in range(steps):
        both = tokens_here[step]
        own = jnp.where(core == 0, both[:, :part], both[:, part:])
        wanted = (place - CAP * step).astype(F32)
        chosen = ((slots[step] == wanted) & (wanted >= 0)).astype(BF)
        main = main + dot(chosen, own, ((0,), (0,)))
        if step == steps - 1:
            last = dot((slots[step] == CAP - 1.0).astype(BF), own, ((0,), (0,)))
    out_ref[:, :part] = main.astype(BF)
    out_ref[:, part:] = ninth_columns(last, part)


def ninth_columns(last, part):
    row = iota((last.shape[0], HALF), 0) % ROWS
    tail = jnp.zeros((last.shape[0], HALF), F32)
    for i in range(part // HALF):
        tail = tail + jnp.where(row == i, last[:, i * HALF : (i + 1) * HALF], 0.0)
    return tail.astype(BF)


def gates_body(routes_ref, gates_ref, out_ref):
    steps, tokens, picks = routes_ref.shape
    rows = out_ref.shape[2]
    experts = rows // ROWS
    out_ref[...] = jnp.zeros(out_ref.shape, BF)
    place = iota((tokens, rows), 1) % ROWS
    experts_of = iota((tokens, experts), 1)
    for step in range(steps):
        routes = routes_ref[step]
        gates = gates_ref[step]
        slots = spread(named_slots(routes, experts), experts)
        gate = jnp.zeros((tokens, experts), F32)
        for k in range(picks):
            gate = gate + jnp.where(routes[:, k : k + 1] == experts_of, gates[:, k : k + 1], 0.0)
        high = gate.astype(BF)
        low = gate - high.astype(F32)
        wanted = (place - CAP * step).astype(F32)
        chosen = (slots == wanted) & (wanted >= 0)
        for n, part in enumerate((spread(high, experts), spread(low, experts))):
            out_ref[n, 16 * step : 16 * step + tokens, :] = jnp.where(chosen, part, 0.0).astype(BF)
            if step == steps - 1:
                for i in range(7):
                    start = 16 * (steps + i)
                    out_ref[n, start : start + tokens, :] = jnp.where(
                        (slots == CAP - 1.0) & (place == i), part, 0.0
                    ).astype(BF)


def slices_body(where_ref, gate_ref, up_ref, down_ref, other_ref, *down_outs):
    chip, core = where_ref[0], where_ref[1]
    units = gate_ref.shape[1]
    part = gate_ref.shape[0] // 8
    for m in range(4):
        offset = pl.multiple_of((2 * (chip ^ m) + 1 - core) * part, HALF)
        rows = slice(m * part, (m + 1) * part)
        other_ref[rows, :units] = gate_ref[pl.ds(offset, part), :]
        other_ref[rows, units:] = up_ref[pl.ds(offset, part), :]
        columns = pl.ds(pl.multiple_of((chip ^ m) * 2 * part, 128), 2 * part)
        down_outs[m][...] = down_ref[:, columns]


def partial_body(where_ref, *refs):
    pieces, (gate_ref, up_ref, other_ref, keep_ref, send_ref) = refs[:4], refs[4:]
    rows = pieces[0].shape[0]
    experts = rows // ROWS
    part = gate_ref.shape[0] // 8
    wide = keep_ref.shape[1]
    chip, core = where_ref[0], where_ref[1]

    def weights(m, start, size):
        offset = pl.multiple_of((2 * (chip ^ m) + core) * part + start, HALF)
        return jnp.concatenate(
            [
                gate_ref[pl.ds(offset, size), :],
                up_ref[pl.ds(offset, size), :],
                other_ref[m * part + start : m * part + start + size, :],
            ],
            axis=1,
        )

    total = jnp.zeros((rows, 2 * wide), F32)
    for m in range(4):
        total = total + dot(pieces[m][:, :part], weights(m, 0, part))
    keep_ref[:rows, :] = total[:, :wide]
    send_ref[:rows, :] = total[:, wide:]
    tail = jnp.concatenate([pieces[m][:, part:] for m in range(4)], axis=1)
    blocks = part // HALF
    source = iota((blocks * experts, rows), 0)
    wanted = (source % experts) * ROWS + source // experts
    chosen = (iota((blocks * experts, rows), 1) == wanted).astype(BF)
    ninth = dot(chosen, tail).astype(BF)
    total = jnp.zeros((experts, 2 * wide), F32)
    for i in range(blocks):
        block_weights = jnp.concatenate([weights(m, i * HALF, HALF) for m in range(4)], axis=0)
        total = total + dot(ninth[i * experts : (i + 1) * experts], block_weights)
    keep_ref[rows:, :] = total[:, :wide]
    send_ref[rows:, :] = total[:, wide:]


def hidden_body(one_ref, two_ref, out_ref):
    units = out_ref.shape[1]
    gate = one_ref[:, :units] + two_ref[:, :units]
    up = one_ref[:, units:] + two_ref[:, units:]
    out_ref[...] = (gate / (1.0 + jnp.exp(-gate)) * up).astype(BF)


def down_body(where_ref, *refs):
    hidden, down, (keep_ref, send_ref) = refs[:4], refs[4:8], refs[8:]
    part = keep_ref.shape[1]
    total = jnp.zeros((hidden[0].shape[0], 2 * part), F32)
    for m in range(4):
        total = total + dot(hidden[m][...], down[m][...])
    first = where_ref[1] == 0
    keep_ref[...] = jnp.where(first, total[:, :part], total[:, part:])
    send_ref[...] = jnp.where(first, total[:, part:], total[:, :part]).astype(BF)


def repack_body(one_ref, two_ref, out_ref):
    rows, part = out_ref.shape[0], one_ref.shape[1]
    experts = rows // ROWS
    total = (one_ref[...] + two_ref[...].astype(F32)).astype(BF)
    out_ref[:, :part] = total[:rows]
    repeat = (iota((rows, experts), 0) // ROWS == iota((rows, experts), 1)).astype(BF)
    out_ref[:, part:] = ninth_columns(dot(repeat, total[rows:]), part)


def combine_body(gates_ref, rows_ref, out_ref):
    steps, tokens, part = out_ref.shape
    values = rows_ref[...]
    total = dot(gates_ref[0], values) + dot(gates_ref[1], values)
    for step in range(steps):
        out = total[16 * step : 16 * step + tokens, :part]
        if step == steps - 1:
            more = [
                total[16 * (steps + i) : 16 * (steps + i) + tokens, part:]
                for i in range(part // HALF)
            ]
            out = out + jnp.concatenate(more, axis=1)
        out_ref[step] = out.astype(BF)


def swap(value, k):
    return lax.ppermute(value, LINE, [(d, d ^ k) for d in range(8)])


def gather_rows(own):
    middle = own.shape[0] // 2
    one, three = swap(own, 2 * 2), swap(own, 3 * 2)
    first = swap(one[:middle], 3 * 2)
    second = swap(three[middle:], 2 * 2)
    return one, three, first, second


def local(
    latent_cache,
    new_latent,
    queries,
    lengths,
    token_rows,
    routes,
    route_gates,
    gate_proj,
    up_proj,
    down_proj,
):
    me = lax.axis_index(LINE)
    experts = lax.axis_size("grp")
    rows = experts * ROWS
    steps, tokens, width = token_rows.shape
    part = width // 8
    units = gate_proj.shape[2]
    where = jnp.stack([me // 2, me % 2]).astype(jnp.int32)

    packed = pl.pallas_call(
        pack_body,
        out_shape=jax.ShapeDtypeStruct((rows, part + HALF), BF),
        in_specs=[SMEM, ANY, ANY],
        out_specs=VMEM,
        scratch_shapes=[
            pltpu.VMEM((steps, tokens, 2 * part), BF),
            pltpu.VMEM(routes.shape, jnp.int32),
            pltpu.SemaphoreType.DMA((2,)),
        ],
        cost_estimate=pl.CostEstimate(flops=10**8, bytes_accessed=10**6, transcendentals=0),
        name="pack",
    )(where, token_rows, routes)
    packed, later = lax.optimization_barrier((packed, where))
    arrived = lax.all_to_all(
        packed.reshape(experts, ROWS, part + HALF), "grp", split_axis=0, concat_axis=0, tiled=True
    ).reshape(rows, part + HALF)

    gate_proj, up_proj = gate_proj.reshape(width, units), up_proj.reshape(width, units)
    other, *down = call(
        slices_body,
        [jax.ShapeDtypeStruct((width // 2, 2 * units), BF)]
        + [jax.ShapeDtypeStruct((units, 2 * part), BF)] * 4,
        [SMEM] + [VMEM] * 3, 10**6, 5 * 10**6, "slices",
    )(later, gate_proj, up_proj, down_proj.reshape(units, width))
    other = swap(other, 1)
    down = [down[0]] + [swap(down[m], 2 * m) for m in range(1, 4)]

    heads = queries.shape[2]
    send, keep = call(
        attend_body, [jax.ShapeDtypeStruct((steps * heads, KL // 2 + 256), F32)] * 2,
        [SMEM, VMEM, VMEM, VMEM], 3 * 10**8, 2 * 10**6, "attend",
    )(
        jnp.stack([later[0] // 2, lengths[0]]),
        queries.reshape(steps * heads, queries.shape[3]),
        latent_cache.reshape(latent_cache.shape[1:]),
        new_latent.reshape(steps, new_latent.shape[2]),
    )
    attention = call(
        merge_body, jax.ShapeDtypeStruct((steps * heads, KL // 2), BF), [VMEM, VMEM],
        10**6, 10**6, "merge",
    )(keep, swap(send, 4))

    gates = call(
        gates_body,
        jax.ShapeDtypeStruct((2, 16 * (steps + part // HALF), rows), BF),
        [VMEM, VMEM], 10**8, 10**6, "gates",
    )(routes, route_gates)

    arrived, other, down, attention, gates = lax.optimization_barrier(
        (arrived, other, down, attention, gates)
    )
    one, three, first, second = gather_rows(arrived)
    two = jnp.concatenate([first, second], axis=0)
    keep, send = call(
        partial_body, [jax.ShapeDtypeStruct((rows + experts, 2 * units), F32)] * 2,
        [SMEM] + [VMEM] * 7, 10**9, 6 * 10**6, "partial",
    )(where, arrived, two, one, three, gate_proj, up_proj, other)
    hidden = call(
        hidden_body, jax.ShapeDtypeStruct((rows + experts, units), BF), [VMEM] * 2,
        10**7, 10**6, "hidden",
    )(keep, swap(send, 1))
    hidden = [hidden] + [swap(hidden, 2 * m) for m in range(1, 4)]
    keep, send = call(
        down_body,
        [
            jax.ShapeDtypeStruct((rows + experts, part), F32),
            jax.ShapeDtypeStruct((rows + experts, part), BF),
        ],
        [SMEM] + [VMEM] * 8, 10**9, 3 * 10**6, "down",
    )(where, *hidden, *down)
    outgoing = call(
        repack_body, jax.ShapeDtypeStruct((rows, part + HALF), BF), [VMEM] * 2,
        10**8, 2 * 10**6, "repack",
    )(keep, swap(send, 1))
    returned = lax.all_to_all(
        outgoing.reshape(experts, ROWS, part + HALF), "grp", split_axis=0, concat_axis=0, tiled=True
    ).reshape(rows, part + HALF)
    moe = call(
        combine_body, jax.ShapeDtypeStruct((steps, tokens, part), BF), [VMEM, VMEM],
        10**8, 10**6, "combine",
    )(gates, returned)
    return attention.reshape(steps, 1, heads, KL // 2), moe


def solution(mesh):
    in_specs = (
        P("grp", "sec", None),
        P(None, "grp", None),
        P(None, "grp", "tp", None),
        P("grp"),
        P(None, "grp", None),
        P(None, "grp", None),
        P(None, "grp", None),
        P("grp", None, ("sec", "tp")),
        P("grp", None, ("sec", "tp")),
        P("grp", ("sec", "tp"), None),
    )
    out_specs = (P(None, "grp", "tp", "sec"), P(None, "grp", ("sec", "tp")))
    return jax.shard_map(local, mesh=mesh, in_specs=in_specs, out_specs=out_specs, check_vma=False)
```

```python
import jax
import jax.numpy as jnp
from jax import lax
from jax.experimental import pallas as pl
from jax.experimental.pallas import tpu as pltpu
from jax.sharding import PartitionSpec as P

CAP = 3
KL = 512
ROWS = 8
HALF = 64

score_scale = 192.0 ** (-0.5)
neg_big = -1e30
BF = jnp.bfloat16
F32 = jnp.float32
LINE = ("sec", "tp")

SMEM = pl.BlockSpec(memory_space=pltpu.SMEM)
VMEM = pl.BlockSpec(memory_space=pltpu.VMEM)
ANY = pl.BlockSpec(memory_space=pl.ANY)


def dot(a, b, dims=((1,), (0,))):
    return lax.dot_general(a, b, (dims, ((), ())), preferred_element_type=F32)


def iota(shape, axis):
    return lax.broadcasted_iota(jnp.int32, shape, axis)


def call(body, out_shape, in_specs, flops, moved, name):
    single = not isinstance(out_shape, (list, tuple))
    return pl.pallas_call(
        body,
        out_shape=out_shape,
        in_specs=in_specs,
        out_specs=VMEM if single else [VMEM] * len(out_shape),
        compiler_params=pltpu.CompilerParams(vmem_limit_bytes=40 * 1024 * 1024),
        cost_estimate=pl.CostEstimate(flops=flops, bytes_accessed=moved, transcendentals=0),
        name=name,
    )


def attend_body(info, q_ref, cache_ref, new_ref, send_ref, keep_ref):
    section, length = info[0], info[1]
    q = q_ref[...]
    rows, local_length = q.shape[0], cache_ref.shape[1]
    steps = new_ref.shape[0]
    heads = rows // steps
    scores = dot(q, cache_ref[...]) * score_scale
    usable = iota((rows, local_length), 1) + section * local_length < length
    scores = jnp.where(usable, scores, neg_big)
    top = jnp.max(scores, axis=1, keepdims=True)
    new_rows = new_ref[...]
    fresh = dot(q, new_rows, ((1,), (1,))) * score_scale
    step_of = iota((rows, steps), 0) // heads
    causal = (iota((rows, steps), 1) <= step_of) & (section == 0)
    fresh = jnp.where(causal, fresh, neg_big)
    top = jnp.maximum(top, jnp.max(fresh, axis=1, keepdims=True))
    weights = jnp.where(usable, jnp.exp(scores - top), 0.0)
    new_weights = jnp.where(causal, jnp.exp(fresh - top), 0.0)
    total = jnp.sum(weights, axis=1, keepdims=True) + jnp.sum(new_weights, axis=1, keepdims=True)
    out = dot(weights.astype(BF), cache_ref[:KL, :], ((1,), (1,)))
    values = new_rows[:, :KL].astype(F32)
    for t in range(steps):
        out = out + new_weights[:, t : t + 1] * values[t : t + 1, :]
    mine = section == 0
    half = KL // 2
    keep_ref[:, :half] = jnp.where(mine, out[:, :half], out[:, half:])
    send_ref[:, :half] = jnp.where(mine, out[:, half:], out[:, :half])
    for ref in (keep_ref, send_ref):
        ref[:, half : half + 128] = jnp.broadcast_to(top, (rows, 128))
        ref[:, half + 128 : half + 256] = jnp.broadcast_to(total, (rows, 128))


def merge_body(one_ref, two_ref, out_ref):
    half = out_ref.shape[1]
    top_one, top_two = one_ref[:, half : half + 1], two_ref[:, half : half + 1]
    top = jnp.maximum(top_one, top_two)
    factor_one, factor_two = jnp.exp(top_one - top), jnp.exp(top_two - top)
    total = (
        one_ref[:, half + 128 : half + 129] * factor_one
        + two_ref[:, half + 128 : half + 129] * factor_two
    )
    out = one_ref[:, :half] * factor_one + two_ref[:, :half] * factor_two
    out_ref[...] = (out / total).astype(BF)


def named_slots(routes, experts):
    tokens, picks = routes.shape
    experts_of = iota((tokens, experts), 1)
    named = jnp.zeros((tokens, experts), F32)
    for k in range(picks):
        named = named + (routes[:, k : k + 1] == experts_of).astype(F32)
    earlier = (iota((tokens, tokens), 1) < iota((tokens, tokens), 0)).astype(BF)
    before = dot(earlier, named.astype(BF))
    return jnp.where(named > 0.5, before, -1.0)


def spread(values, experts):
    rows = experts * ROWS
    repeat = (iota((experts, rows), 1) // ROWS == iota((experts, rows), 0)).astype(BF)
    return dot(values.astype(BF), repeat)


def pack_body(where_ref, tokens_ref, routes_ref, out_ref):
    chip, core = where_ref[0], where_ref[1]
    rows = out_ref.shape[0]
    experts = rows // ROWS
    steps, picks, tokens = routes_ref.shape
    part = tokens_ref.shape[2] // 8
    columns = pl.ds(pl.multiple_of(chip * 2 * part, 128), 2 * part)
    place = iota((rows, tokens), 0) % ROWS
    repeat = (iota((rows, experts), 0) // ROWS == iota((rows, experts), 1)).astype(BF)
    earlier = (iota((tokens, tokens), 0) < iota((tokens, tokens), 1)).astype(BF)
    experts_of = iota((experts, tokens), 0)
    main = jnp.zeros((rows, part), F32)
    for step in range(steps):
        named = jnp.zeros((experts, tokens), F32)
        for k in range(picks):
            named = named + (routes_ref[step, k : k + 1, :] == experts_of).astype(F32)
        before = dot(named.astype(BF), earlier)
        slots = dot(repeat, jnp.where(named > 0.5, before, -1.0).astype(BF))
        both = tokens_ref[step, :, columns]
        own = jnp.where(core == 0, both[:, :part], both[:, part:])
        wanted = (place - CAP * step).astype(F32)
        chosen = ((slots == wanted) & (wanted >= 0)).astype(BF)
        main = main + dot(chosen, own)
        if step == steps - 1:
            last = dot((slots == CAP - 1.0).astype(BF), own)
    out_ref[:, :part] = main.astype(BF)
    out_ref[:, part:] = ninth_columns(last, part)


def ninth_columns(last, part):
    row = iota((last.shape[0], HALF), 0) % ROWS
    tail = jnp.zeros((last.shape[0], HALF), F32)
    for i in range(part // HALF):
        tail = tail + jnp.where(row == i, last[:, i * HALF : (i + 1) * HALF], 0.0)
    return tail.astype(BF)


def gates_body(routes_ref, gates_ref, out_ref):
    steps, tokens, picks = routes_ref.shape
    rows = out_ref.shape[2]
    experts = rows // ROWS
    out_ref[...] = jnp.zeros(out_ref.shape, BF)
    place = iota((tokens, rows), 1) % ROWS
    experts_of = iota((tokens, experts), 1)
    for step in range(steps):
        routes = routes_ref[step]
        gates = gates_ref[step]
        slots = spread(named_slots(routes, experts), experts)
        gate = jnp.zeros((tokens, experts), F32)
        for k in range(picks):
            gate = gate + jnp.where(routes[:, k : k + 1] == experts_of, gates[:, k : k + 1], 0.0)
        high = gate.astype(BF)
        low = gate - high.astype(F32)
        wanted = (place - CAP * step).astype(F32)
        chosen = (slots == wanted) & (wanted >= 0)
        for n, part in enumerate((spread(high, experts), spread(low, experts))):
            out_ref[n, 16 * step : 16 * step + tokens, :] = jnp.where(chosen, part, 0.0).astype(BF)
            if step == steps - 1:
                for i in range(7):
                    start = 16 * (steps + i)
                    out_ref[n, start : start + tokens, :] = jnp.where(
                        (slots == CAP - 1.0) & (place == i), part, 0.0
                    ).astype(BF)


def slices_body(where_ref, gate_ref, up_ref, down_ref, other_ref, *down_outs):
    chip, core = where_ref[0], where_ref[1]
    units = gate_ref.shape[1]
    part = gate_ref.shape[0] // 8
    for m in range(4):
        offset = pl.multiple_of((2 * (chip ^ m) + 1 - core) * part, HALF)
        rows = slice(m * part, (m + 1) * part)
        other_ref[rows, :units] = gate_ref[pl.ds(offset, part), :]
        other_ref[rows, units:] = up_ref[pl.ds(offset, part), :]
        columns = pl.ds(pl.multiple_of((chip ^ m) * 2 * part, 128), 2 * part)
        down_outs[m][...] = down_ref[:, columns]


def partial_body(where_ref, *refs):
    own, (gate_ref, up_ref, other_ref, keep_ref, send_ref) = refs[0], refs[7:]
    halves = [[own]] + [refs[m : m + 2] for m in (1, 3, 5)]
    pieces = [jnp.concatenate([h[...] for h in m], axis=0) for m in halves]
    rows = own.shape[0]
    experts = rows // ROWS
    part = gate_ref.shape[0] // 8
    wide = keep_ref.shape[1]
    chip, core = where_ref[0], where_ref[1]

    def weights(m, start, size):
        offset = pl.multiple_of((2 * (chip ^ m) + core) * part + start, HALF)
        return jnp.concatenate(
            [
                gate_ref[pl.ds(offset, size), :],
                up_ref[pl.ds(offset, size), :],
                other_ref[m * part + start : m * part + start + size, :],
            ],
            axis=1,
        )

    total = jnp.zeros((rows, 2 * wide), F32)
    for m in range(4):
        total = total + dot(pieces[m][:, :part], weights(m, 0, part))
    keep_ref[:rows, :] = total[:, :wide]
    send_ref[:rows, :] = total[:, wide:]
    tail = jnp.concatenate([pieces[m][:, part:] for m in range(4)], axis=1)
    blocks = part // HALF
    source = iota((blocks * experts, rows), 0)
    wanted = (source % experts) * ROWS + source // experts
    chosen = (iota((blocks * experts, rows), 1) == wanted).astype(BF)
    ninth = dot(chosen, tail).astype(BF)
    total = jnp.zeros((experts, 2 * wide), F32)
    for i in range(blocks):
        block_weights = jnp.concatenate([weights(m, i * HALF, HALF) for m in range(4)], axis=0)
        total = total + dot(ninth[i * experts : (i + 1) * experts], block_weights)
    keep_ref[rows:, :] = total[:, :wide]
    send_ref[rows:, :] = total[:, wide:]


def hidden_body(one_ref, two_ref, out_ref):
    units = out_ref.shape[1]
    gate = one_ref[:, :units] + two_ref[:, :units]
    up = one_ref[:, units:] + two_ref[:, units:]
    out_ref[...] = (gate / (1.0 + jnp.exp(-gate)) * up).astype(BF)


def down_body(where_ref, *refs):
    hidden, down, (keep_ref, send_ref) = refs[:4], refs[4:8], refs[8:]
    part = keep_ref.shape[1]
    total = jnp.zeros((hidden[0].shape[0], 2 * part), F32)
    for m in range(4):
        total = total + dot(hidden[m][...], down[m][...])
    first = where_ref[1] == 0
    keep_ref[...] = jnp.where(first, total[:, :part], total[:, part:])
    send_ref[:, :part] = jnp.where(first, total[:, part:], total[:, :part]).astype(BF)
    send_ref[:, part:] = jnp.zeros((total.shape[0], HALF), BF)


def repack_body(one_ref, two_ref, out_ref):
    rows, part = out_ref.shape[0], one_ref.shape[1]
    experts = rows // ROWS
    total = (one_ref[...] + two_ref[:, :part].astype(F32)).astype(BF)
    out_ref[:, :part] = total[:rows]
    repeat = (iota((rows, experts), 0) // ROWS == iota((rows, experts), 1)).astype(BF)
    out_ref[:, part:] = ninth_columns(dot(repeat, total[rows:]), part)


def combine_body(gates_ref, rows_ref, out_ref):
    steps, tokens, part = out_ref.shape
    values = rows_ref[...]
    total = dot(gates_ref[0], values) + dot(gates_ref[1], values)
    for step in range(steps):
        out = total[16 * step : 16 * step + tokens, :part]
        if step == steps - 1:
            more = [
                total[16 * (steps + i) : 16 * (steps + i) + tokens, part:]
                for i in range(part // HALF)
            ]
            out = out + jnp.concatenate(more, axis=1)
        out_ref[step] = out.astype(BF)


def swap(value, k):
    return lax.ppermute(value, LINE, [(d, d ^ k) for d in range(8)])


def gather_rows(own):
    middle = own.shape[0] // 2
    upper, lower = own[:middle], own[middle:]
    two_upper, three_lower = swap(upper, 4), swap(lower, 6)
    two_lower, three_upper = swap(lower, 4), swap(upper, 6)
    return swap(two_upper, 6), swap(three_lower, 4), two_upper, two_lower, three_upper, three_lower


def local(
    latent_cache,
    new_latent,
    queries,
    lengths,
    token_rows,
    routes,
    route_gates,
    gate_proj,
    up_proj,
    down_proj,
):
    me = lax.axis_index(LINE)
    experts = lax.axis_size("grp")
    rows = experts * ROWS
    steps, tokens, width = token_rows.shape
    part = width // 8
    units = gate_proj.shape[2]
    section = lax.axis_index("sec").astype(jnp.int32)
    where = jnp.stack([me // 2, me % 2]).astype(jnp.int32)

    packed = call(
        pack_body, jax.ShapeDtypeStruct((rows, part + HALF), BF), [SMEM, VMEM, VMEM],
        10**8, 10**6, "pack",
    )(where, token_rows, jnp.swapaxes(routes, 1, 2))
    packed, later = lax.optimization_barrier((packed, where))
    arrived = lax.all_to_all(
        packed.reshape(experts, ROWS, part + HALF), "grp", split_axis=0, concat_axis=0, tiled=True
    ).reshape(rows, part + HALF)

    gate_proj, up_proj = gate_proj.reshape(width, units), up_proj.reshape(width, units)
    other, *down = call(
        slices_body,
        [jax.ShapeDtypeStruct((width // 2, 2 * units), BF)]
        + [jax.ShapeDtypeStruct((units, 2 * part), BF)] * 4,
        [SMEM] + [VMEM] * 3, 10**6, 5 * 10**6, "slices",
    )(later, gate_proj, up_proj, down_proj.reshape(units, width))
    other = swap(other, 1)
    down = [down[0]] + [swap(down[m], 2 * m) for m in range(1, 4)]

    arrived, other, down = lax.optimization_barrier((arrived, other, down))
    keep, send = call(
        partial_body, [jax.ShapeDtypeStruct((rows + experts, 2 * units), F32)] * 2,
        [SMEM] + [VMEM] * 10, 10**9, 6 * 10**6, "partial",
    )(where, arrived, *gather_rows(arrived), gate_proj, up_proj, other)
    hidden = call(
        hidden_body, jax.ShapeDtypeStruct((rows + experts, units), BF), [VMEM] * 2,
        10**7, 10**6, "hidden",
    )(keep, swap(send, 1))
    two = swap(hidden, 4)
    hidden = [hidden, swap(two, 6), two, swap(hidden, 6)]
    keep, send = call(
        down_body,
        [
            jax.ShapeDtypeStruct((rows + experts, part), F32),
            jax.ShapeDtypeStruct((rows + experts, part + HALF), BF),
        ],
        [SMEM] + [VMEM] * 8, 10**9, 3 * 10**6, "down",
    )(where, *hidden, *down)
    outgoing = call(
        repack_body, jax.ShapeDtypeStruct((rows, part + HALF), BF), [VMEM] * 2,
        10**8, 2 * 10**6, "repack",
    )(keep, swap(send, 1))
    outgoing, info, gates = lax.optimization_barrier(
        (outgoing, jnp.stack([section, lengths[0]]), route_gates)
    )
    returned = lax.all_to_all(
        outgoing.reshape(experts, ROWS, part + HALF), "grp", split_axis=0, concat_axis=0, tiled=True
    ).reshape(rows, part + HALF)

    heads = queries.shape[2]
    send, keep = call(
        attend_body, [jax.ShapeDtypeStruct((steps * heads, KL // 2 + 256), F32)] * 2,
        [SMEM, VMEM, VMEM, VMEM], 3 * 10**8, 2 * 10**6, "attend",
    )(
        info,
        queries.reshape(steps * heads, queries.shape[3]),
        latent_cache[0].T,
        new_latent.reshape(steps, new_latent.shape[2]),
    )
    attention = call(
        merge_body, jax.ShapeDtypeStruct((steps * heads, KL // 2), BF), [VMEM, VMEM],
        10**6, 10**6, "merge",
    )(keep, swap(send, 4))
    gates = call(
        gates_body,
        jax.ShapeDtypeStruct((2, 16 * (steps + part // HALF), rows), BF),
        [VMEM, VMEM], 10**8, 10**6, "gates",
    )(routes, gates)
    moe = call(
        combine_body, jax.ShapeDtypeStruct((steps, tokens, part), BF), [VMEM, VMEM],
        10**8, 10**6, "combine",
    )(gates, returned)
    return attention.reshape(steps, 1, heads, KL // 2), moe


def solution(mesh):
    in_specs = (
        P("grp", "sec", None),
        P(None, "grp", None),
        P(None, "grp", "tp", None),
        P("grp"),
        P(None, "grp", None),
        P(None, "grp", None),
        P(None, "grp", None),
        P("grp", None, ("sec", "tp")),
        P("grp", None, ("sec", "tp")),
        P("grp", ("sec", "tp"), None),
    )
    out_specs = (P(None, "grp", "tp", "sec"), P(None, "grp", ("sec", "tp")))
    return jax.shard_map(local, mesh=mesh, in_specs=in_specs, out_specs=out_specs, check_vma=False)
```

```python
import jax
import jax.numpy as jnp
from jax import lax
from jax.experimental import pallas as pl
from jax.experimental.pallas import tpu as pltpu
from jax.sharding import PartitionSpec as P

CAP = 3
KL = 512
ROWS = 8
HALF = 64

score_scale = 192.0 ** (-0.5)
neg_big = -1e30
BF = jnp.bfloat16
F32 = jnp.float32
LINE = ("sec", "tp")

SMEM = pl.BlockSpec(memory_space=pltpu.SMEM)
VMEM = pl.BlockSpec(memory_space=pltpu.VMEM)
HBM = pl.BlockSpec(memory_space=pltpu.HBM)


def dot(a, b, dims=((1,), (0,))):
    return lax.dot_general(a, b, (dims, ((), ())), preferred_element_type=F32)


def iota(shape, axis):
    return lax.broadcasted_iota(jnp.int32, shape, axis)


def call(body, out_shape, in_specs, flops, moved, name):
    single = not isinstance(out_shape, (list, tuple))
    return pl.pallas_call(
        body,
        out_shape=out_shape,
        in_specs=in_specs,
        out_specs=VMEM if single else [VMEM] * len(out_shape),
        compiler_params=pltpu.CompilerParams(vmem_limit_bytes=40 * 1024 * 1024),
        cost_estimate=pl.CostEstimate(flops=flops, bytes_accessed=moved, transcendentals=0),
        name=name,
    )


def attend_body(length_ref, q_ref, cache_ref, new_ref, send_ref, keep_ref):
    section, length = lax.axis_index("sec").astype(jnp.int32), length_ref[0]
    q = q_ref[...]
    rows, local_length = q.shape[0], cache_ref.shape[1]
    steps = new_ref.shape[0]
    heads = rows // steps
    scores = dot(q, cache_ref[...]) * score_scale
    usable = iota((rows, local_length), 1) + section * local_length < length
    scores = jnp.where(usable, scores, neg_big)
    top = jnp.max(scores, axis=1, keepdims=True)
    new_rows = new_ref[...]
    fresh = dot(q, new_rows, ((1,), (1,))) * score_scale
    step_of = iota((rows, steps), 0) // heads
    causal = (iota((rows, steps), 1) <= step_of) & (section == 0)
    fresh = jnp.where(causal, fresh, neg_big)
    top = jnp.maximum(top, jnp.max(fresh, axis=1, keepdims=True))
    weights = jnp.where(usable, jnp.exp(scores - top), 0.0)
    new_weights = jnp.where(causal, jnp.exp(fresh - top), 0.0)
    total = jnp.sum(weights, axis=1, keepdims=True) + jnp.sum(new_weights, axis=1, keepdims=True)
    out = dot(weights.astype(BF), cache_ref[:KL, :], ((1,), (1,)))
    values = new_rows[:, :KL].astype(F32)
    for t in range(steps):
        out = out + new_weights[:, t : t + 1] * values[t : t + 1, :]
    mine = section == 0
    half = KL // 2
    keep_ref[:, :half] = jnp.where(mine, out[:, :half], out[:, half:])
    send_ref[:, :half] = jnp.where(mine, out[:, half:], out[:, :half])
    for ref in (keep_ref, send_ref):
        ref[:, half : half + 128] = jnp.broadcast_to(top, (rows, 128))
        ref[:, half + 128 : half + 256] = jnp.broadcast_to(total, (rows, 128))


def merge_body(one_ref, two_ref, out_ref):
    half = out_ref.shape[1]
    top_one, top_two = one_ref[:, half : half + 1], two_ref[:, half : half + 1]
    top = jnp.maximum(top_one, top_two)
    factor_one, factor_two = jnp.exp(top_one - top), jnp.exp(top_two - top)
    total = (
        one_ref[:, half + 128 : half + 129] * factor_one
        + two_ref[:, half + 128 : half + 129] * factor_two
    )
    out = one_ref[:, :half] * factor_one + two_ref[:, :half] * factor_two
    out_ref[...] = (out / total).astype(BF)


def place_here():
    return lax.axis_index(LINE).astype(jnp.int32)


def sources(d):
    core = d % 2
    return d, d ^ (4 + 2 * core), d ^ (5 + 2 * core), d ^ 2


def permute(value, target):
    return lax.ppermute(value, LINE, [(d, target(d)) for d in range(8)])


def swap(value, k):
    return permute(value, lambda d: d ^ k)


def gather(own):
    near = permute(own, lambda d: d ^ (4 + 2 * (d % 2)))
    crossed = permute(own, lambda d: d ^ (7 - 2 * (d % 2)))
    return own, near, crossed, permute(near, lambda d: d ^ (6 - 2 * (d % 2)))


def named_slots(routes, experts):
    tokens, picks = routes.shape
    experts_of = iota((tokens, experts), 1)
    named = jnp.zeros((tokens, experts), F32)
    for k in range(picks):
        named = named + (routes[:, k : k + 1] == experts_of).astype(F32)
    earlier = (iota((tokens, tokens), 1) < iota((tokens, tokens), 0)).astype(BF)
    before = dot(earlier, named.astype(BF))
    return jnp.where(named > 0.5, before, -1.0)


def spread(values, experts):
    rows = experts * ROWS
    repeat = (iota((experts, rows), 1) // ROWS == iota((experts, rows), 0)).astype(BF)
    return dot(values.astype(BF), repeat)


def pack_body(tokens_ref, routes_ref, out_ref, tokens_here, routes_here, sems):
    here = place_here()
    rows = out_ref.shape[0]
    experts = rows // ROWS
    steps, picks, tokens = routes_ref.shape
    part = tokens_ref.shape[2] // 8
    columns = pl.ds(pl.multiple_of((here // 2) * 2 * part, 128), 2 * part)
    fetch_routes = pltpu.make_async_copy(routes_ref, routes_here, sems.at[0])
    fetch_tokens = pltpu.make_async_copy(tokens_ref.at[:, :, columns], tokens_here, sems.at[1])
    fetch_routes.start()
    fetch_tokens.start()
    place = iota((rows, tokens), 0) % ROWS
    repeat = (iota((rows, experts), 0) // ROWS == iota((rows, experts), 1)).astype(BF)
    earlier = (iota((tokens, tokens), 0) < iota((tokens, tokens), 1)).astype(BF)
    experts_of = iota((experts, tokens), 0)
    fetch_routes.wait()
    slots = []
    for step in range(steps):
        named = jnp.zeros((experts, tokens), F32)
        for k in range(picks):
            named = named + (routes_here[step, k : k + 1, :] == experts_of).astype(F32)
        before = dot(named.astype(BF), earlier)
        slots.append(dot(repeat, jnp.where(named > 0.5, before, -1.0).astype(BF)))
    fetch_tokens.wait()
    main = jnp.zeros((rows, part), F32)
    for step in range(steps):
        both = tokens_here[step]
        own = jnp.where(here % 2 == 0, both[:, :part], both[:, part:])
        wanted = (place - CAP * step).astype(F32)
        chosen = ((slots[step] == wanted) & (wanted >= 0)).astype(BF)
        main = main + dot(chosen, own)
    last = dot((slots[-1] == CAP - 1.0).astype(BF), own)
    out_ref[:, :part] = main.astype(BF)
    out_ref[:, part:] = ninth_columns(last, part)


def ninth_columns(last, part):
    row = iota((last.shape[0], HALF), 0) % ROWS
    tail = jnp.zeros((last.shape[0], HALF), F32)
    for i in range(part // HALF):
        tail = tail + jnp.where(row == i, last[:, i * HALF : (i + 1) * HALF], 0.0)
    return tail.astype(BF)


def gates_body(routes_ref, gates_ref, out_ref):
    steps, tokens, picks = routes_ref.shape
    rows = out_ref.shape[2]
    experts = rows // ROWS
    out_ref[...] = jnp.zeros(out_ref.shape, BF)
    place = iota((tokens, rows), 1) % ROWS
    experts_of = iota((tokens, experts), 1)
    for step in range(steps):
        routes = routes_ref[step]
        gates = gates_ref[step]
        slots = spread(named_slots(routes, experts), experts)
        gate = jnp.zeros((tokens, experts), F32)
        for k in range(picks):
            gate = gate + jnp.where(routes[:, k : k + 1] == experts_of, gates[:, k : k + 1], 0.0)
        high = gate.astype(BF)
        low = gate - high.astype(F32)
        wanted = (place - CAP * step).astype(F32)
        chosen = (slots == wanted) & (wanted >= 0)
        for n, part in enumerate((spread(high, experts), spread(low, experts))):
            out_ref[n, 16 * step : 16 * step + tokens, :] = jnp.where(chosen, part, 0.0).astype(BF)
            if step == steps - 1:
                for i in range(7):
                    start = 16 * (steps + i)
                    out_ref[n, start : start + tokens, :] = jnp.where(
                        (slots == CAP - 1.0) & (place == i), part, 0.0
                    ).astype(BF)


def slices_body(gate_ref, up_ref, down_ref, other_ref, *down_outs):
    here = place_here()
    units = gate_ref.shape[1]
    part = gate_ref.shape[0] // 8
    core = here % 2
    for m, source in enumerate(sources(here ^ 1)):
        offset = pl.multiple_of(source * part, HALF)
        rows = slice(m * part, (m + 1) * part)
        other_ref[rows, :units] = gate_ref[pl.ds(offset, part), :]
        other_ref[rows, units:] = up_ref[pl.ds(offset, part), :]
    targets = here, here ^ (4 + 2 * core), here ^ (7 - 2 * core), here ^ 2
    for target, out in zip(targets, down_outs):
        out[...] = down_ref[:, pl.ds(pl.multiple_of((target // 2) * 2 * part, 128), 2 * part)]


def partial_body(*refs):
    pieces, (gate_ref, up_ref, other_ref, keep_ref, send_ref) = refs[:4], refs[4:]
    rows = pieces[0].shape[0]
    experts = rows // ROWS
    part = gate_ref.shape[0] // 8
    wide = keep_ref.shape[1]
    blocks_of = sources(place_here())

    def weights(m, start, size):
        offset = pl.multiple_of(blocks_of[m] * part + start, HALF)
        return jnp.concatenate(
            [
                gate_ref[pl.ds(offset, size), :],
                up_ref[pl.ds(offset, size), :],
                other_ref[m * part + start : m * part + start + size, :],
            ],
            axis=1,
        )

    total = jnp.zeros((rows, 2 * wide), F32)
    for m in range(4):
        total = total + dot(pieces[m][:, :part], weights(m, 0, part))
    keep_ref[:rows, :] = total[:, :wide]
    send_ref[:rows, :] = total[:, wide:]
    tail = jnp.concatenate([pieces[m][:, part:] for m in range(4)], axis=1)
    blocks = part // HALF
    source = iota((blocks * experts, rows), 0)
    wanted = (source % experts) * ROWS + source // experts
    chosen = (iota((blocks * experts, rows), 1) == wanted).astype(BF)
    ninth = dot(chosen, tail).astype(BF)
    total = jnp.zeros((experts, 2 * wide), F32)
    for i in range(blocks):
        block_weights = jnp.concatenate([weights(m, i * HALF, HALF) for m in range(4)], axis=0)
        total = total + dot(ninth[i * experts : (i + 1) * experts], block_weights)
    keep_ref[rows:, :] = total[:, :wide]
    send_ref[rows:, :] = total[:, wide:]


def hidden_body(one_ref, two_ref, out_ref):
    units = out_ref.shape[1]
    gate = one_ref[:, :units] + two_ref[:, :units]
    up = one_ref[:, units:] + two_ref[:, units:]
    out_ref[...] = (gate / (1.0 + jnp.exp(-gate)) * up).astype(BF)


def down_body(*refs):
    hidden, down, (keep_ref, send_ref) = refs[:4], refs[4:8], refs[8:]
    part = keep_ref.shape[1]
    total = jnp.zeros((hidden[0].shape[0], 2 * part), F32)
    for m in range(4):
        total = total + dot(hidden[m][...], down[m][...])
    first = place_here() % 2 == 0
    keep_ref[...] = jnp.where(first, total[:, :part], total[:, part:])
    send_ref[:, :part] = jnp.where(first, total[:, part:], total[:, :part]).astype(BF)
    send_ref[:, part:] = jnp.zeros((total.shape[0], HALF), BF)


def repack_body(one_ref, two_ref, out_ref):
    rows, part = out_ref.shape[0], one_ref.shape[1]
    experts = rows // ROWS
    total = (one_ref[...] + two_ref[:, :part].astype(F32)).astype(BF)
    out_ref[:, :part] = total[:rows]
    repeat = (iota((rows, experts), 0) // ROWS == iota((rows, experts), 1)).astype(BF)
    out_ref[:, part:] = ninth_columns(dot(repeat, total[rows:]), part)


def combine_body(gates_ref, rows_ref, out_ref):
    steps, tokens, part = out_ref.shape
    values = rows_ref[...]
    total = dot(gates_ref[0], values) + dot(gates_ref[1], values)
    for step in range(steps):
        out = total[16 * step : 16 * step + tokens, :part]
        if step == steps - 1:
            more = [
                total[16 * (steps + i) : 16 * (steps + i) + tokens, part:]
                for i in range(part // HALF)
            ]
            out = out + jnp.concatenate(more, axis=1)
        out_ref[step] = out.astype(BF)


def local(
    latent_cache,
    new_latent,
    queries,
    lengths,
    token_rows,
    routes,
    route_gates,
    gate_proj,
    up_proj,
    down_proj,
):
    experts = lax.axis_size("grp")
    rows = experts * ROWS
    steps, tokens, width = token_rows.shape
    part = width // 8
    units = gate_proj.shape[2]
    packed = pl.pallas_call(
        pack_body,
        out_shape=jax.ShapeDtypeStruct((rows, part + HALF), BF),
        in_specs=[HBM, HBM],
        out_specs=VMEM,
        scratch_shapes=[
            pltpu.VMEM((steps, tokens, 2 * part), BF),
            pltpu.VMEM((steps, routes.shape[2], tokens), jnp.int32),
            pltpu.SemaphoreType.DMA((2,)),
        ],
        cost_estimate=pl.CostEstimate(flops=10**8, bytes_accessed=10**6, transcendentals=0),
        name="pack",
    )(token_rows, jnp.swapaxes(routes, 1, 2))
    packed, down_proj = lax.optimization_barrier((packed, down_proj))
    arrived = lax.all_to_all(
        packed.reshape(experts, ROWS, part + HALF), "grp", split_axis=0, concat_axis=0, tiled=True
    ).reshape(rows, part + HALF)

    gate_proj, up_proj = gate_proj.reshape(width, units), up_proj.reshape(width, units)
    other, *down = call(
        slices_body,
        [jax.ShapeDtypeStruct((width // 2, 2 * units), BF)]
        + [jax.ShapeDtypeStruct((units, 2 * part), BF)] * 4,
        [VMEM] * 3, 10**6, 5 * 10**6, "slices",
    )(gate_proj, up_proj, down_proj.reshape(units, width))
    other = swap(other, 1)
    down = [
        down[0],
        permute(down[1], lambda d: d ^ (4 + 2 * (d % 2))),
        permute(down[2], lambda d: d ^ (7 - 2 * (d % 2))),
        swap(down[3], 2),
    ]

    arrived, other, down = lax.optimization_barrier((arrived, other, down))
    keep, send = call(
        partial_body, [jax.ShapeDtypeStruct((rows + experts, 2 * units), F32)] * 2,
        [VMEM] * 7, 10**9, 6 * 10**6, "partial",
    )(*gather(arrived), gate_proj, up_proj, other)
    hidden = call(
        hidden_body, jax.ShapeDtypeStruct((rows + experts, units), BF), [VMEM] * 2,
        10**7, 10**6, "hidden",
    )(keep, swap(send, 1))
    keep, send = call(
        down_body,
        [
            jax.ShapeDtypeStruct((rows + experts, part), F32),
            jax.ShapeDtypeStruct((rows + experts, part + HALF), BF),
        ],
        [VMEM] * 8, 10**9, 3 * 10**6, "down",
    )(*gather(hidden), *down)
    outgoing = call(
        repack_body, jax.ShapeDtypeStruct((rows, part + HALF), BF), [VMEM] * 2,
        10**8, 2 * 10**6, "repack",
    )(keep, swap(send, 1))
    outgoing, lengths, gates = lax.optimization_barrier((outgoing, lengths, route_gates))
    returned = lax.all_to_all(
        outgoing.reshape(experts, ROWS, part + HALF), "grp", split_axis=0, concat_axis=0, tiled=True
    ).reshape(rows, part + HALF)

    heads = queries.shape[2]
    send, keep = call(
        attend_body, [jax.ShapeDtypeStruct((steps * heads, KL // 2 + 256), F32)] * 2,
        [SMEM, VMEM, VMEM, VMEM], 3 * 10**8, 2 * 10**6, "attend",
    )(
        lengths,
        queries.reshape(steps * heads, queries.shape[3]),
        latent_cache[0].T,
        new_latent.reshape(steps, new_latent.shape[2]),
    )
    attention = call(
        merge_body, jax.ShapeDtypeStruct((steps * heads, KL // 2), BF), [VMEM, VMEM],
        10**6, 10**6, "merge",
    )(keep, swap(send, 4))
    gates = call(
        gates_body,
        jax.ShapeDtypeStruct((2, 16 * (steps + part // HALF), rows), BF),
        [VMEM, VMEM], 10**8, 10**6, "gates",
    )(routes, gates)
    moe = call(
        combine_body, jax.ShapeDtypeStruct((steps, tokens, part), BF), [VMEM, VMEM],
        10**8, 10**6, "combine",
    )(gates, returned)
    return attention.reshape(steps, 1, heads, KL // 2), moe


def solution(mesh):
    in_specs = (
        P("grp", "sec", None),
        P(None, "grp", None),
        P(None, "grp", "tp", None),
        P("grp"),
        P(None, "grp", None),
        P(None, "grp", None),
        P(None, "grp", None),
        P("grp", None, ("sec", "tp")),
        P("grp", None, ("sec", "tp")),
        P("grp", ("sec", "tp"), None),
    )
    out_specs = (P(None, "grp", "tp", "sec"), P(None, "grp", ("sec", "tp")))
    return jax.shard_map(local, mesh=mesh, in_specs=in_specs, out_specs=out_specs, check_vma=False)
```

```python
import jax
import jax.numpy as jnp
from jax import lax
from jax.experimental import pallas as pl
from jax.experimental.pallas import tpu as pltpu
from jax.sharding import PartitionSpec as P

CAP = 3
KL = 512
ROWS = 8
HALF = 64

score_scale = 192.0 ** (-0.5)
neg_big = -1e30
BF = jnp.bfloat16
F32 = jnp.float32
LINE = ("sec", "tp")

SMEM = pl.BlockSpec(memory_space=pltpu.SMEM)
VMEM = pl.BlockSpec(memory_space=pltpu.VMEM)
HBM = pl.BlockSpec(memory_space=pltpu.HBM)


def dot(a, b, dims=((1,), (0,))):
    return lax.dot_general(a, b, (dims, ((), ())), preferred_element_type=F32)


def iota(shape, axis):
    return lax.broadcasted_iota(jnp.int32, shape, axis)


def call(body, out_shape, in_specs, flops, moved, name):
    single = not isinstance(out_shape, (list, tuple))
    return pl.pallas_call(
        body,
        out_shape=out_shape,
        in_specs=in_specs,
        out_specs=VMEM if single else [VMEM] * len(out_shape),
        compiler_params=pltpu.CompilerParams(vmem_limit_bytes=20 * 1024 * 1024),
        cost_estimate=pl.CostEstimate(flops=flops, bytes_accessed=moved, transcendentals=0),
        name=name,
    )


def attend_body(_, length_ref, q_ref, cache_ref, new_ref, send_ref, keep_ref):
    section, length = lax.axis_index("sec").astype(jnp.int32), length_ref[0]
    q = q_ref[...]
    rows, local_length = q.shape[0], cache_ref.shape[1]
    steps = new_ref.shape[0]
    heads = rows // steps
    scores = dot(q, cache_ref[...]) * score_scale
    usable = iota((rows, local_length), 1) + section * local_length < length
    scores = jnp.where(usable, scores, neg_big)
    top = jnp.max(scores, axis=1, keepdims=True)
    new_rows = new_ref[...]
    fresh = dot(q, new_rows, ((1,), (1,))) * score_scale
    step_of = iota((rows, steps), 0) // heads
    causal = (iota((rows, steps), 1) <= step_of) & (section == 0)
    fresh = jnp.where(causal, fresh, neg_big)
    top = jnp.maximum(top, jnp.max(fresh, axis=1, keepdims=True))
    weights = jnp.where(usable, jnp.exp(scores - top), 0.0)
    new_weights = jnp.where(causal, jnp.exp(fresh - top), 0.0)
    total = jnp.sum(weights, axis=1, keepdims=True) + jnp.sum(new_weights, axis=1, keepdims=True)
    out = dot(weights.astype(BF), cache_ref[:KL, :], ((1,), (1,)))
    values = new_rows[:, :KL].astype(F32)
    for t in range(steps):
        out = out + new_weights[:, t : t + 1] * values[t : t + 1, :]
    mine = section == 0
    half = KL // 2
    keep_ref[:, :half] = jnp.where(mine, out[:, :half], out[:, half:])
    send_ref[:, :half] = jnp.where(mine, out[:, half:], out[:, :half])
    for ref in (keep_ref, send_ref):
        ref[:, half : half + 128] = jnp.broadcast_to(top, (rows, 128))
        ref[:, half + 128 : half + 256] = jnp.broadcast_to(total, (rows, 128))


def merge_body(one_ref, two_ref, out_ref):
    half = out_ref.shape[1]
    top_one, top_two = one_ref[:, half : half + 1], two_ref[:, half : half + 1]
    top = jnp.maximum(top_one, top_two)
    factor_one, factor_two = jnp.exp(top_one - top), jnp.exp(top_two - top)
    total = (
        one_ref[:, half + 128 : half + 129] * factor_one
        + two_ref[:, half + 128 : half + 129] * factor_two
    )
    out = one_ref[:, :half] * factor_one + two_ref[:, :half] * factor_two
    out_ref[...] = (out / total).astype(BF)


def place_here():
    return lax.axis_index(LINE).astype(jnp.int32)


def sources(d):
    core = d % 2
    return d, d ^ (4 + 2 * core), d ^ (5 + 2 * core), d ^ 2


def permute(value, target):
    return lax.ppermute(value, LINE, [(d, target(d)) for d in range(8)])


def swap(value, k):
    return permute(value, lambda d: d ^ k)


def to_near(value):
    return permute(value, lambda d: d ^ (4 + 2 * (d % 2)))


def to_crossed(value):
    return permute(value, lambda d: d ^ (7 - 2 * (d % 2)))


def onward(value):
    return permute(value, lambda d: d ^ (6 - 2 * (d % 2)))


def named_slots(routes, experts):
    tokens, picks = routes.shape
    experts_of = iota((tokens, experts), 1)
    named = jnp.zeros((tokens, experts), F32)
    for k in range(picks):
        named = named + (routes[:, k : k + 1] == experts_of).astype(F32)
    earlier = (iota((tokens, tokens), 1) < iota((tokens, tokens), 0)).astype(BF)
    before = dot(earlier, named.astype(BF))
    return jnp.where(named > 0.5, before, -1.0)


def spread(values, experts):
    rows = experts * ROWS
    repeat = (iota((experts, rows), 1) // ROWS == iota((experts, rows), 0)).astype(BF)
    return dot(values.astype(BF), repeat)


def pack_body(tokens_ref, routes_ref, out_ref, tokens_here, routes_here, sems):
    here = place_here()
    rows = out_ref.shape[0]
    experts = rows // ROWS
    steps, picks, tokens = routes_ref.shape
    part = tokens_ref.shape[2] // 8
    columns = pl.ds(pl.multiple_of((here // 2) * 2 * part, 128), 2 * part)
    fetch_routes = pltpu.make_async_copy(routes_ref, routes_here, sems.at[0])
    fetch_tokens = pltpu.make_async_copy(tokens_ref.at[:, :, columns], tokens_here, sems.at[1])
    fetch_routes.start()
    fetch_tokens.start()
    place = iota((rows, tokens), 0) % ROWS
    repeat = (iota((rows, experts), 0) // ROWS == iota((rows, experts), 1)).astype(BF)
    earlier = (iota((tokens, tokens), 0) < iota((tokens, tokens), 1)).astype(BF)
    experts_of = iota((experts, tokens), 0)
    fetch_routes.wait()
    slots = []
    for step in range(steps):
        named = jnp.zeros((experts, tokens), F32)
        for k in range(picks):
            named = named + (routes_here[step, k : k + 1, :] == experts_of).astype(F32)
        before = dot(named.astype(BF), earlier)
        slots.append(dot(repeat, jnp.where(named > 0.5, before, -1.0).astype(BF)))
    fetch_tokens.wait()
    main = jnp.zeros((rows, part), F32)
    for step in range(steps):
        both = tokens_here[step]
        own = jnp.where(here % 2 == 0, both[:, :part], both[:, part:])
        wanted = (place - CAP * step).astype(F32)
        chosen = ((slots[step] == wanted) & (wanted >= 0)).astype(BF)
        main = main + dot(chosen, own)
    last = dot((slots[-1] == CAP - 1.0).astype(BF), own)
    out_ref[:, :part] = main.astype(BF)
    out_ref[:, part:] = ninth_columns(last, part)


def ninth_columns(last, part):
    row = iota((last.shape[0], HALF), 0) % ROWS
    tail = jnp.zeros((last.shape[0], HALF), F32)
    for i in range(part // HALF):
        tail = tail + jnp.where(row == i, last[:, i * HALF : (i + 1) * HALF], 0.0)
    return tail.astype(BF)


def gates_body(_, routes_ref, gates_ref, out_ref):
    steps, tokens, picks = routes_ref.shape
    rows = out_ref.shape[2]
    experts = rows // ROWS
    out_ref[...] = jnp.zeros(out_ref.shape, BF)
    place = iota((tokens, rows), 1) % ROWS
    experts_of = iota((tokens, experts), 1)
    for step in range(steps):
        routes = routes_ref[step]
        gates = gates_ref[step]
        slots = spread(named_slots(routes, experts), experts)
        gate = jnp.zeros((tokens, experts), F32)
        for k in range(picks):
            gate = gate + jnp.where(routes[:, k : k + 1] == experts_of, gates[:, k : k + 1], 0.0)
        high = gate.astype(BF)
        low = gate - high.astype(F32)
        wanted = (place - CAP * step).astype(F32)
        chosen = (slots == wanted) & (wanted >= 0)
        for n, part in enumerate((spread(high, experts), spread(low, experts))):
            out_ref[n, 16 * step : 16 * step + tokens, :] = jnp.where(chosen, part, 0.0).astype(BF)
            if step == steps - 1:
                for i in range(7):
                    start = 16 * (steps + i)
                    out_ref[n, start : start + tokens, :] = jnp.where(
                        (slots == CAP - 1.0) & (place == i), part, 0.0
                    ).astype(BF)


def slices_body(_, gate_ref, up_ref, down_ref, other_ref, own_ref, near_ref, crossed_ref):
    here = place_here()
    units = gate_ref.shape[1]
    part = gate_ref.shape[0] // 8
    core = here % 2

    def columns(target):
        return down_ref[:, pl.ds(pl.multiple_of((target // 2) * 2 * part, 128), 2 * part)]

    for m, source in enumerate(sources(here ^ 1)):
        offset = pl.multiple_of(source * part, HALF)
        rows = slice(m * part, (m + 1) * part)
        other_ref[rows, :units] = gate_ref[pl.ds(offset, part), :]
        other_ref[rows, units:] = up_ref[pl.ds(offset, part), :]
    own_ref[...] = columns(here)
    near_ref[:units, :] = columns(here ^ (4 + 2 * core))
    near_ref[units:, :] = columns(here ^ 2)
    crossed_ref[...] = columns(here ^ (7 - 2 * core))


def partial_body(*refs):
    pieces, (gate_ref, up_ref, other_ref, keep_ref, send_ref) = refs[:4], refs[4:]
    rows = pieces[0].shape[0]
    experts = rows // ROWS
    part = gate_ref.shape[0] // 8
    wide = keep_ref.shape[1]
    blocks_of = sources(place_here())

    def weights(m, start, size):
        offset = pl.multiple_of(blocks_of[m] * part + start, HALF)
        return jnp.concatenate(
            [
                gate_ref[pl.ds(offset, size), :],
                up_ref[pl.ds(offset, size), :],
                other_ref[m * part + start : m * part + start + size, :],
            ],
            axis=1,
        )

    total = jnp.zeros((rows, wide), F32)
    for m in range(4):
        total = total + dot(pieces[m][:, :part], weights(m, 0, part))
    keep_ref[:rows, :] = total
    send_ref[:rows, :] = total.astype(BF)
    tail = jnp.concatenate([pieces[m][:, part:] for m in range(4)], axis=1)
    blocks = part // HALF
    source = iota((blocks * experts, rows), 0)
    wanted = (source % experts) * ROWS + source // experts
    chosen = (iota((blocks * experts, rows), 1) == wanted).astype(BF)
    ninth = dot(chosen, tail).astype(BF)
    total = jnp.zeros((experts, wide), F32)
    for i in range(blocks):
        block_weights = jnp.concatenate([weights(m, i * HALF, HALF) for m in range(4)], axis=0)
        total = total + dot(ninth[i * experts : (i + 1) * experts], block_weights)
    keep_ref[rows:, :] = total
    send_ref[rows:, :] = total.astype(BF)


def hidden_body(mine_ref, other_ref, out_ref):
    units = out_ref.shape[1] // 2
    for half in range(2):
        mine, other = 2 * half * units, 2 * (1 - half) * units
        gate = mine_ref[:, mine : mine + units] + other_ref[:, other : other + units].astype(F32)
        mine, other = mine + units, other + units
        up = mine_ref[:, mine : mine + units] + other_ref[:, other : other + units].astype(F32)
        out_ref[:, half * units : (half + 1) * units] = (
            gate / (1.0 + jnp.exp(-gate)) * up
        ).astype(BF)


def down_body(chip_ref, near_ref, far_ref, own_w, near_w, crossed_w, far_w, keep_ref, send_ref):
    part, units = keep_ref.shape[1], own_w.shape[0]
    total = dot(chip_ref[:, :units], own_w[...]) + dot(near_ref[:, :units], near_w[:units, :])
    total = total + dot(near_ref[:, units:], crossed_w[...]) + dot(far_ref[...], far_w[...])
    first = place_here() % 2 == 0
    keep_ref[...] = jnp.where(first, total[:, :part], total[:, part:])
    send_ref[:, :part] = jnp.where(first, total[:, part:], total[:, :part]).astype(BF)
    send_ref[:, part:] = jnp.zeros((total.shape[0], HALF), BF)


def repack_body(one_ref, two_ref, out_ref):
    rows, part = out_ref.shape[0], one_ref.shape[1]
    experts = rows // ROWS
    total = (one_ref[...] + two_ref[:, :part].astype(F32)).astype(BF)
    out_ref[:, :part] = total[:rows]
    repeat = (iota((rows, experts), 0) // ROWS == iota((rows, experts), 1)).astype(BF)
    out_ref[:, part:] = ninth_columns(dot(repeat, total[rows:]), part)


def combine_body(gates_ref, rows_ref, out_ref):
    steps, tokens, part = out_ref.shape
    values = rows_ref[...]
    total = dot(gates_ref[0], values) + dot(gates_ref[1], values)
    for step in range(steps):
        out = total[16 * step : 16 * step + tokens, :part]
        if step == steps - 1:
            more = [
                total[16 * (steps + i) : 16 * (steps + i) + tokens, part:]
                for i in range(part // HALF)
            ]
            out = out + jnp.concatenate(more, axis=1)
        out_ref[step] = out.astype(BF)


def local(
    latent_cache,
    new_latent,
    queries,
    lengths,
    token_rows,
    routes,
    route_gates,
    gate_proj,
    up_proj,
    down_proj,
):
    experts = lax.axis_size("grp")
    rows = experts * ROWS
    steps, tokens, width = token_rows.shape
    part = width // 8
    units = gate_proj.shape[2]
    packed = pl.pallas_call(
        pack_body,
        out_shape=jax.ShapeDtypeStruct((rows, part + HALF), BF),
        in_specs=[HBM, HBM],
        out_specs=VMEM,
        scratch_shapes=[
            pltpu.VMEM((steps, tokens, 2 * part), BF),
            pltpu.VMEM((steps, routes.shape[2], tokens), jnp.int32),
            pltpu.SemaphoreType.DMA((2,)),
        ],
        cost_estimate=pl.CostEstimate(flops=10**8, bytes_accessed=10**6, transcendentals=0),
        name="pack",
    )(token_rows, jnp.swapaxes(routes, 1, 2))
    arrived = lax.all_to_all(
        packed.reshape(experts, ROWS, part + HALF), "grp", split_axis=0, concat_axis=0, tiled=True
    ).reshape(rows, part + HALF)

    gate_proj, up_proj = gate_proj.reshape(width, units), up_proj.reshape(width, units)
    other, own_down, near_down, crossed_down = call(
        slices_body,
        [
            jax.ShapeDtypeStruct((width // 2, 2 * units), BF),
            jax.ShapeDtypeStruct((units, 2 * part), BF),
            jax.ShapeDtypeStruct((2 * units, 2 * part), BF),
            jax.ShapeDtypeStruct((units, 2 * part), BF),
        ],
        [HBM] + [VMEM] * 3, 10**6, 5 * 10**6, "slices",
    )(packed, gate_proj, up_proj, down_proj.reshape(units, width))
    other = swap(other, 1)
    near_down, crossed_down = to_near(near_down), to_crossed(crossed_down)
    arrived, near_down, crossed_down = lax.optimization_barrier(
        (arrived, near_down, crossed_down)
    )
    far_down = onward(near_down[units:])

    near = to_near(arrived)
    crossed = to_crossed(arrived)
    keep, send = call(
        partial_body,
        [
            jax.ShapeDtypeStruct((rows + experts, 4 * units), F32),
            jax.ShapeDtypeStruct((rows + experts, 4 * units), BF),
        ],
        [VMEM] * 7, 10**9, 6 * 10**6, "partial",
    )(arrived, near, crossed, onward(near), gate_proj, up_proj, other)
    hidden = call(
        hidden_body, jax.ShapeDtypeStruct((rows + experts, 2 * units), BF), [VMEM] * 2,
        10**7, 10**6, "hidden",
    )(keep, swap(send, 1))
    near = to_near(hidden)
    keep, send = call(
        down_body,
        [
            jax.ShapeDtypeStruct((rows + experts, part), F32),
            jax.ShapeDtypeStruct((rows + experts, part + HALF), BF),
        ],
        [VMEM] * 7, 10**9, 3 * 10**6, "down",
    )(hidden, near, onward(near[:, :units]), own_down, near_down, crossed_down, far_down)
    outgoing = call(
        repack_body, jax.ShapeDtypeStruct((rows, part + HALF), BF), [VMEM] * 2,
        10**8, 2 * 10**6, "repack",
    )(keep, swap(send, 1))
    returned = lax.all_to_all(
        outgoing.reshape(experts, ROWS, part + HALF), "grp", split_axis=0, concat_axis=0, tiled=True
    ).reshape(rows, part + HALF)

    heads = queries.shape[2]
    send, keep = call(
        attend_body, [jax.ShapeDtypeStruct((steps * heads, KL // 2 + 256), F32)] * 2,
        [HBM, SMEM, VMEM, VMEM, VMEM], 3 * 10**8, 2 * 10**6, "attend",
    )(
        outgoing,
        lengths,
        queries.reshape(steps * heads, queries.shape[3]),
        latent_cache[0].T,
        new_latent.reshape(steps, new_latent.shape[2]),
    )
    attention = call(
        merge_body, jax.ShapeDtypeStruct((steps * heads, KL // 2), BF), [VMEM, VMEM],
        10**6, 10**6, "merge",
    )(keep, swap(send, 4))
    gates = call(
        gates_body,
        jax.ShapeDtypeStruct((2, 16 * (steps + part // HALF), rows), BF),
        [HBM, VMEM, VMEM], 10**8, 10**6, "gates",
    )(outgoing, routes, route_gates)
    moe = call(
        combine_body, jax.ShapeDtypeStruct((steps, tokens, part), BF), [VMEM, VMEM],
        10**8, 10**6, "combine",
    )(gates, returned)
    return attention.reshape(steps, 1, heads, KL // 2), moe


def solution(mesh):
    in_specs = (
        P("grp", "sec", None),
        P(None, "grp", None),
        P(None, "grp", "tp", None),
        P("grp"),
        P(None, "grp", None),
        P(None, "grp", None),
        P(None, "grp", None),
        P("grp", None, ("sec", "tp")),
        P("grp", None, ("sec", "tp")),
        P("grp", ("sec", "tp"), None),
    )
    out_specs = (P(None, "grp", "tp", "sec"), P(None, "grp", ("sec", "tp")))
    return jax.shard_map(local, mesh=mesh, in_specs=in_specs, out_specs=out_specs, check_vma=False)
```

```python
import jax
import jax.numpy as jnp
from jax import lax
from jax.experimental import pallas as pl
from jax.experimental.pallas import tpu as pltpu
from jax.sharding import PartitionSpec as P

CAP = 3
KL = 512
ROWS = 8
HALF = 64

score_scale = 192.0 ** (-0.5)
neg_big = -1e30
BF = jnp.bfloat16
F32 = jnp.float32
LINE = ("sec", "tp")

SMEM = pl.BlockSpec(memory_space=pltpu.SMEM)
VMEM = pl.BlockSpec(memory_space=pltpu.VMEM)
HBM = pl.BlockSpec(memory_space=pltpu.HBM)


def dot(a, b, dims=((1,), (0,))):
    return lax.dot_general(a, b, (dims, ((), ())), preferred_element_type=F32)


def iota(shape, axis):
    return lax.broadcasted_iota(jnp.int32, shape, axis)


def call(body, out_shape, in_specs, flops, moved, name):
    single = not isinstance(out_shape, (list, tuple))
    return pl.pallas_call(
        body,
        out_shape=out_shape,
        in_specs=in_specs,
        out_specs=VMEM if single else [VMEM] * len(out_shape),
        compiler_params=pltpu.CompilerParams(vmem_limit_bytes=20 * 1024 * 1024),
        cost_estimate=pl.CostEstimate(flops=flops, bytes_accessed=moved, transcendentals=0),
        name=name,
    )


def attend_body(_, length_ref, q_ref, cache_ref, new_ref, send_ref, keep_ref):
    section, length = lax.axis_index("sec").astype(jnp.int32), length_ref[0]
    q = q_ref[...]
    rows, local_length = q.shape[0], cache_ref.shape[1]
    steps = new_ref.shape[0]
    heads = rows // steps
    scores = dot(q, cache_ref[...]) * score_scale
    usable = iota((rows, local_length), 1) + section * local_length < length
    scores = jnp.where(usable, scores, neg_big)
    top = jnp.max(scores, axis=1, keepdims=True)
    new_rows = new_ref[...]
    fresh = dot(q, new_rows, ((1,), (1,))) * score_scale
    step_of = iota((rows, steps), 0) // heads
    causal = (iota((rows, steps), 1) <= step_of) & (section == 0)
    fresh = jnp.where(causal, fresh, neg_big)
    top = jnp.maximum(top, jnp.max(fresh, axis=1, keepdims=True))
    weights = jnp.where(usable, jnp.exp(scores - top), 0.0)
    new_weights = jnp.where(causal, jnp.exp(fresh - top), 0.0)
    total = jnp.sum(weights, axis=1, keepdims=True) + jnp.sum(new_weights, axis=1, keepdims=True)
    out = dot(weights.astype(BF), cache_ref[:KL, :], ((1,), (1,)))
    values = new_rows[:, :KL].astype(F32)
    for t in range(steps):
        out = out + new_weights[:, t : t + 1] * values[t : t + 1, :]
    mine = section == 0
    half = KL // 2
    keep_ref[:, :half] = jnp.where(mine, out[:, :half], out[:, half:])
    send_ref[:, :half] = jnp.where(mine, out[:, half:], out[:, :half])
    for ref in (keep_ref, send_ref):
        ref[:, half : half + 128] = jnp.broadcast_to(top, (rows, 128))
        ref[:, half + 128 : half + 256] = jnp.broadcast_to(total, (rows, 128))


def merge_body(one_ref, two_ref, out_ref):
    half = out_ref.shape[1]
    top_one, top_two = one_ref[:, half : half + 1], two_ref[:, half : half + 1]
    top = jnp.maximum(top_one, top_two)
    factor_one, factor_two = jnp.exp(top_one - top), jnp.exp(top_two - top)
    total = (
        one_ref[:, half + 128 : half + 129] * factor_one
        + two_ref[:, half + 128 : half + 129] * factor_two
    )
    out = one_ref[:, :half] * factor_one + two_ref[:, :half] * factor_two
    out_ref[...] = (out / total).astype(BF)


def place_here():
    return lax.axis_index(LINE).astype(jnp.int32)


def sources(d):
    core = d % 2
    return d, d ^ (4 + 2 * core), d ^ (5 + 2 * core), d ^ 2


def permute(value, target):
    return lax.ppermute(value, LINE, [(d, target(d)) for d in range(8)])


def swap(value, k):
    return permute(value, lambda d: d ^ k)


def to_near(value):
    return permute(value, lambda d: d ^ (4 + 2 * (d % 2)))


def to_crossed(value):
    return permute(value, lambda d: d ^ (7 - 2 * (d % 2)))


def onward(value):
    return permute(value, lambda d: d ^ (6 - 2 * (d % 2)))


def gather(own):
    near = to_near(own)
    return own, near, to_crossed(own), onward(near)


def named_slots(routes, experts):
    tokens, picks = routes.shape
    experts_of = iota((tokens, experts), 1)
    named = jnp.zeros((tokens, experts), F32)
    for k in range(picks):
        named = named + (routes[:, k : k + 1] == experts_of).astype(F32)
    earlier = (iota((tokens, tokens), 1) < iota((tokens, tokens), 0)).astype(BF)
    before = dot(earlier, named.astype(BF))
    return jnp.where(named > 0.5, before, -1.0)


def spread(values, experts):
    rows = experts * ROWS
    repeat = (iota((experts, rows), 1) // ROWS == iota((experts, rows), 0)).astype(BF)
    return dot(values.astype(BF), repeat)


def pack_body(tokens_ref, routes_ref, out_ref, mark_ref, tokens_here, routes_here, sems):
    here = place_here()
    rows = out_ref.shape[0]
    experts = rows // ROWS
    steps, picks, tokens = routes_ref.shape
    part = tokens_ref.shape[2] // 8
    columns = pl.ds(pl.multiple_of((here // 2) * 2 * part, 128), 2 * part)
    fetch_routes = pltpu.make_async_copy(routes_ref, routes_here, sems.at[0])
    fetch_tokens = pltpu.make_async_copy(tokens_ref.at[:, :, columns], tokens_here, sems.at[1])
    fetch_routes.start()
    fetch_tokens.start()
    place = iota((rows, tokens), 0) % ROWS
    repeat = (iota((rows, experts), 0) // ROWS == iota((rows, experts), 1)).astype(BF)
    earlier = (iota((tokens, tokens), 0) < iota((tokens, tokens), 1)).astype(BF)
    experts_of = iota((experts, tokens), 0)
    fetch_routes.wait()
    slots = []
    for step in range(steps):
        named = jnp.zeros((experts, tokens), F32)
        for k in range(picks):
            named = named + (routes_here[step, k : k + 1, :] == experts_of).astype(F32)
        before = dot(named.astype(BF), earlier)
        slots.append(dot(repeat, jnp.where(named > 0.5, before, -1.0).astype(BF)))
    fetch_tokens.wait()
    main = jnp.zeros((rows, part), F32)
    for step in range(steps):
        both = tokens_here[step]
        own = jnp.where(here % 2 == 0, both[:, :part], both[:, part:])
        wanted = (place - CAP * step).astype(F32)
        chosen = ((slots[step] == wanted) & (wanted >= 0)).astype(BF)
        main = main + dot(chosen, own)
    last = dot((slots[-1] == CAP - 1.0).astype(BF), own)
    out_ref[:, :part] = main.astype(BF)
    out_ref[:, part:] = ninth_columns(last, part)
    mark_ref[...] = jnp.zeros(mark_ref.shape, F32)


def ninth_columns(last, part):
    row = iota((last.shape[0], HALF), 0) % ROWS
    tail = jnp.zeros((last.shape[0], HALF), F32)
    for i in range(part // HALF):
        tail = tail + jnp.where(row == i, last[:, i * HALF : (i + 1) * HALF], 0.0)
    return tail.astype(BF)


def gates_body(_, routes_ref, gates_ref, out_ref):
    steps, tokens, picks = routes_ref.shape
    rows = out_ref.shape[2]
    experts = rows // ROWS
    out_ref[...] = jnp.zeros(out_ref.shape, BF)
    place = iota((tokens, rows), 1) % ROWS
    experts_of = iota((tokens, experts), 1)
    for step in range(steps):
        routes = routes_ref[step]
        gates = gates_ref[step]
        slots = spread(named_slots(routes, experts), experts)
        gate = jnp.zeros((tokens, experts), F32)
        for k in range(picks):
            gate = gate + jnp.where(routes[:, k : k + 1] == experts_of, gates[:, k : k + 1], 0.0)
        high = gate.astype(BF)
        low = gate - high.astype(F32)
        wanted = (place - CAP * step).astype(F32)
        chosen = (slots == wanted) & (wanted >= 0)
        for n, part in enumerate((spread(high, experts), spread(low, experts))):
            out_ref[n, 16 * step : 16 * step + tokens, :] = jnp.where(chosen, part, 0.0).astype(BF)
            if step == steps - 1:
                for i in range(7):
                    start = 16 * (steps + i)
                    out_ref[n, start : start + tokens, :] = jnp.where(
                        (slots == CAP - 1.0) & (place == i), part, 0.0
                    ).astype(BF)


def down_slices_body(_, down_ref, near_ref, crossed_ref):
    here = place_here()
    core = here % 2
    units, wide = crossed_ref.shape

    def columns(target):
        return down_ref[:, pl.ds(pl.multiple_of((target // 2) * wide, 128), wide)]

    near_ref[:units, :] = columns(here ^ (4 + 2 * core))
    near_ref[units:, :] = columns(here ^ 2)
    crossed_ref[...] = columns(here ^ (7 - 2 * core))


def other_slices_body(_, gate_ref, up_ref, other_ref):
    units = gate_ref.shape[1]
    part = gate_ref.shape[0] // 8
    for m, source in enumerate(sources(place_here() ^ 1)):
        offset = pl.multiple_of(source * part, HALF)
        rows = slice(m * part, (m + 1) * part)
        other_ref[rows, :units] = gate_ref[pl.ds(offset, part), :]
        other_ref[rows, units:] = up_ref[pl.ds(offset, part), :]


def partial_body(*refs):
    pieces, (gate_ref, up_ref, other_ref, keep_ref, send_ref) = refs[:4], refs[5:]
    rows = pieces[0].shape[0]
    experts = rows // ROWS
    part = gate_ref.shape[0] // 8
    wide = keep_ref.shape[1]
    blocks_of = sources(place_here())

    def weights(m, start, size):
        offset = pl.multiple_of(blocks_of[m] * part + start, HALF)
        return jnp.concatenate(
            [
                gate_ref[pl.ds(offset, size), :],
                up_ref[pl.ds(offset, size), :],
                other_ref[m * part + start : m * part + start + size, :],
            ],
            axis=1,
        )

    total = jnp.zeros((rows, 2 * wide), F32)
    for m in range(4):
        total = total + dot(pieces[m][:, :part], weights(m, 0, part))
    keep_ref[:rows, :] = total[:, :wide]
    send_ref[:rows, :] = total[:, wide:]
    tail = jnp.concatenate([pieces[m][:, part:] for m in range(4)], axis=1)
    blocks = part // HALF
    source = iota((blocks * experts, rows), 0)
    wanted = (source % experts) * ROWS + source // experts
    chosen = (iota((blocks * experts, rows), 1) == wanted).astype(BF)
    ninth = dot(chosen, tail).astype(BF)
    total = jnp.zeros((experts, 2 * wide), F32)
    for i in range(blocks):
        block_weights = jnp.concatenate([weights(m, i * HALF, HALF) for m in range(4)], axis=0)
        total = total + dot(ninth[i * experts : (i + 1) * experts], block_weights)
    keep_ref[rows:, :] = total[:, :wide]
    send_ref[rows:, :] = total[:, wide:]


def hidden_body(one_ref, two_ref, out_ref):
    units = out_ref.shape[1]
    gate = one_ref[:, :units] + two_ref[:, :units]
    up = one_ref[:, units:] + two_ref[:, units:]
    out_ref[...] = (gate / (1.0 + jnp.exp(-gate)) * up).astype(BF)


def down_body(own_h, near_h, crossed_h, far_h, down_ref, near_w, crossed_w, far_w, keep_ref, send_ref):
    part, units = keep_ref.shape[1], down_ref.shape[0]
    here = pl.ds(pl.multiple_of((place_here() // 2) * 2 * part, 128), 2 * part)
    total = dot(own_h[...], down_ref[:, here]) + dot(near_h[...], near_w[:units, :])
    total = total + dot(crossed_h[...], crossed_w[...]) + dot(far_h[...], far_w[...])
    first = place_here() % 2 == 0
    keep_ref[...] = jnp.where(first, total[:, :part], total[:, part:])
    send_ref[:, :part] = jnp.where(first, total[:, part:], total[:, :part]).astype(BF)
    send_ref[:, part:] = jnp.zeros((total.shape[0], HALF), BF)


def repack_body(one_ref, two_ref, out_ref):
    rows, part = out_ref.shape[0], one_ref.shape[1]
    experts = rows // ROWS
    total = (one_ref[...] + two_ref[:, :part].astype(F32)).astype(BF)
    out_ref[:, :part] = total[:rows]
    repeat = (iota((rows, experts), 0) // ROWS == iota((rows, experts), 1)).astype(BF)
    out_ref[:, part:] = ninth_columns(dot(repeat, total[rows:]), part)


def combine_body(gates_ref, rows_ref, out_ref):
    steps, tokens, part = out_ref.shape
    values = rows_ref[...]
    total = dot(gates_ref[0], values) + dot(gates_ref[1], values)
    for step in range(steps):
        out = total[16 * step : 16 * step + tokens, :part]
        if step == steps - 1:
            more = [
                total[16 * (steps + i) : 16 * (steps + i) + tokens, part:]
                for i in range(part // HALF)
            ]
            out = out + jnp.concatenate(more, axis=1)
        out_ref[step] = out.astype(BF)


def local(
    latent_cache,
    new_latent,
    queries,
    lengths,
    token_rows,
    routes,
    route_gates,
    gate_proj,
    up_proj,
    down_proj,
):
    experts = lax.axis_size("grp")
    rows = experts * ROWS
    steps, tokens, width = token_rows.shape
    part = width // 8
    units = gate_proj.shape[2]
    packed, mark = pl.pallas_call(
        pack_body,
        out_shape=[
            jax.ShapeDtypeStruct((rows, part + HALF), BF),
            jax.ShapeDtypeStruct((8, 128), F32),
        ],
        in_specs=[HBM, HBM],
        out_specs=[VMEM, VMEM],
        scratch_shapes=[
            pltpu.VMEM((steps, tokens, 2 * part), BF),
            pltpu.VMEM((steps, routes.shape[2], tokens), jnp.int32),
            pltpu.SemaphoreType.DMA((2,)),
        ],
        cost_estimate=pl.CostEstimate(flops=10**8, bytes_accessed=10**6, transcendentals=0),
        name="pack",
    )(token_rows, jnp.swapaxes(routes, 1, 2))
    arrived = lax.all_to_all(
        packed.reshape(experts, ROWS, part + HALF), "grp", split_axis=0, concat_axis=0, tiled=True
    ).reshape(rows, part + HALF)

    gate_proj, up_proj = gate_proj.reshape(width, units), up_proj.reshape(width, units)
    down_proj = down_proj.reshape(units, width)
    near_down, crossed_down = call(
        down_slices_body,
        [
            jax.ShapeDtypeStruct((2 * units, 2 * part), BF),
            jax.ShapeDtypeStruct((units, 2 * part), BF),
        ],
        [VMEM, VMEM], 10**6, 2 * 10**6, "down_slices",
    )(mark, down_proj)
    near_down, crossed_down = to_near(near_down), to_crossed(crossed_down)
    arrived, near_down, crossed_down = lax.optimization_barrier(
        (arrived, near_down, crossed_down)
    )
    other = call(
        other_slices_body, jax.ShapeDtypeStruct((width // 2, 2 * units), BF),
        [VMEM] * 3, 10**6, 4 * 10**6, "other_slices",
    )(arrived, gate_proj, up_proj)
    other = swap(other, 1)
    far_down = onward(near_down[units:])

    keep, send = call(
        partial_body, [jax.ShapeDtypeStruct((rows + experts, 2 * units), F32)] * 2,
        [VMEM] * 4 + [HBM] + [VMEM] * 3, 10**9, 6 * 10**6, "partial",
    )(*gather(arrived), far_down, gate_proj, up_proj, other)
    hidden = call(
        hidden_body, jax.ShapeDtypeStruct((rows + experts, units), BF), [VMEM] * 2,
        10**7, 10**6, "hidden",
    )(keep, swap(send, 1))
    keep, send = call(
        down_body,
        [
            jax.ShapeDtypeStruct((rows + experts, part), F32),
            jax.ShapeDtypeStruct((rows + experts, part + HALF), BF),
        ],
        [VMEM] * 8, 10**9, 3 * 10**6, "down",
    )(*gather(hidden), down_proj, near_down, crossed_down, far_down)
    outgoing = call(
        repack_body, jax.ShapeDtypeStruct((rows, part + HALF), BF), [VMEM] * 2,
        10**8, 2 * 10**6, "repack",
    )(keep, swap(send, 1))
    returned = lax.all_to_all(
        outgoing.reshape(experts, ROWS, part + HALF), "grp", split_axis=0, concat_axis=0, tiled=True
    ).reshape(rows, part + HALF)

    heads = queries.shape[2]
    send, keep = call(
        attend_body, [jax.ShapeDtypeStruct((steps * heads, KL // 2 + 256), F32)] * 2,
        [HBM, SMEM, VMEM, VMEM, VMEM], 3 * 10**8, 2 * 10**6, "attend",
    )(
        outgoing,
        lengths,
        queries.reshape(steps * heads, queries.shape[3]),
        latent_cache[0].T,
        new_latent.reshape(steps, new_latent.shape[2]),
    )
    attention = call(
        merge_body, jax.ShapeDtypeStruct((steps * heads, KL // 2), BF), [VMEM, VMEM],
        10**6, 10**6, "merge",
    )(keep, swap(send, 4))
    gates = call(
        gates_body,
        jax.ShapeDtypeStruct((2, 16 * (steps + part // HALF), rows), BF),
        [HBM, VMEM, VMEM], 10**8, 10**6, "gates",
    )(outgoing, routes, route_gates)
    moe = call(
        combine_body, jax.ShapeDtypeStruct((steps, tokens, part), BF), [VMEM, VMEM],
        10**8, 10**6, "combine",
    )(gates, returned)
    return attention.reshape(steps, 1, heads, KL // 2), moe


def solution(mesh):
    in_specs = (
        P("grp", "sec", None),
        P(None, "grp", None),
        P(None, "grp", "tp", None),
        P("grp"),
        P(None, "grp", None),
        P(None, "grp", None),
        P(None, "grp", None),
        P("grp", None, ("sec", "tp")),
        P("grp", None, ("sec", "tp")),
        P("grp", ("sec", "tp"), None),
    )
    out_specs = (P(None, "grp", "tp", "sec"), P(None, "grp", ("sec", "tp")))
    return jax.shard_map(local, mesh=mesh, in_specs=in_specs, out_specs=out_specs, check_vma=False)
```

```python
import jax
import jax.numpy as jnp
from jax import lax
from jax.experimental import pallas as pl
from jax.experimental.pallas import tpu as pltpu
from jax.sharding import PartitionSpec as P

CAP = 3
KL = 512
ROWS = 8
HALF = 64

score_scale = 192.0 ** (-0.5)
neg_big = -1e30
BF = jnp.bfloat16
F32 = jnp.float32
LINE = ("sec", "tp")

SMEM = pl.BlockSpec(memory_space=pltpu.SMEM)
VMEM = pl.BlockSpec(memory_space=pltpu.VMEM)
HBM = pl.BlockSpec(memory_space=pltpu.HBM)


def dot(a, b, dims=((1,), (0,))):
    return lax.dot_general(a, b, (dims, ((), ())), preferred_element_type=F32)


def iota(shape, axis):
    return lax.broadcasted_iota(jnp.int32, shape, axis)


def call(body, out_shape, in_specs, flops, moved, name):
    single = not isinstance(out_shape, (list, tuple))
    return pl.pallas_call(
        body,
        out_shape=out_shape,
        in_specs=in_specs,
        out_specs=VMEM if single else [VMEM] * len(out_shape),
        compiler_params=pltpu.CompilerParams(vmem_limit_bytes=20 * 1024 * 1024),
        cost_estimate=pl.CostEstimate(flops=flops, bytes_accessed=moved, transcendentals=0),
        name=name,
    )


def attend_body(_, length_ref, q_ref, cache_ref, new_ref, send_ref, keep_ref):
    section, length = lax.axis_index("sec").astype(jnp.int32), length_ref[0]
    q = q_ref[...]
    rows, local_length = q.shape[0], cache_ref.shape[1]
    steps = new_ref.shape[0]
    heads = rows // steps
    scores = dot(q, cache_ref[...]) * score_scale
    usable = iota((rows, local_length), 1) + section * local_length < length
    scores = jnp.where(usable, scores, neg_big)
    top = jnp.max(scores, axis=1, keepdims=True)
    new_rows = new_ref[...]
    fresh = dot(q, new_rows, ((1,), (1,))) * score_scale
    step_of = iota((rows, steps), 0) // heads
    causal = (iota((rows, steps), 1) <= step_of) & (section == 0)
    fresh = jnp.where(causal, fresh, neg_big)
    top = jnp.maximum(top, jnp.max(fresh, axis=1, keepdims=True))
    weights = jnp.where(usable, jnp.exp(scores - top), 0.0)
    new_weights = jnp.where(causal, jnp.exp(fresh - top), 0.0)
    total = jnp.sum(weights, axis=1, keepdims=True) + jnp.sum(new_weights, axis=1, keepdims=True)
    out = dot(weights.astype(BF), cache_ref[:KL, :], ((1,), (1,)))
    values = new_rows[:, :KL].astype(F32)
    for t in range(steps):
        out = out + new_weights[:, t : t + 1] * values[t : t + 1, :]
    mine = section == 0
    half = KL // 2
    keep_ref[:, :half] = jnp.where(mine, out[:, :half], out[:, half:])
    send_ref[:, :half] = jnp.where(mine, out[:, half:], out[:, :half])
    for ref in (keep_ref, send_ref):
        ref[:, half : half + 128] = jnp.broadcast_to(top, (rows, 128))
        ref[:, half + 128 : half + 256] = jnp.broadcast_to(total, (rows, 128))


def merge_body(one_ref, two_ref, out_ref):
    half = out_ref.shape[1]
    top_one, top_two = one_ref[:, half : half + 1], two_ref[:, half : half + 1]
    top = jnp.maximum(top_one, top_two)
    factor_one, factor_two = jnp.exp(top_one - top), jnp.exp(top_two - top)
    total = (
        one_ref[:, half + 128 : half + 129] * factor_one
        + two_ref[:, half + 128 : half + 129] * factor_two
    )
    out = one_ref[:, :half] * factor_one + two_ref[:, :half] * factor_two
    out_ref[...] = (out / total).astype(BF)


def place_here():
    return lax.axis_index(LINE).astype(jnp.int32)


def sources(d):
    core = d % 2
    return d, d ^ (4 + 2 * core), d ^ (5 + 2 * core), d ^ 2


def permute(value, target):
    return lax.ppermute(value, LINE, [(d, target(d)) for d in range(8)])


def swap(value, k):
    return permute(value, lambda d: d ^ k)


def to_near(value):
    return permute(value, lambda d: d ^ (4 + 2 * (d % 2)))


def to_crossed(value):
    return permute(value, lambda d: d ^ (7 - 2 * (d % 2)))


def onward(value):
    return permute(value, lambda d: d ^ (6 - 2 * (d % 2)))


def gather(own):
    near = to_near(own)
    return own, near, to_crossed(own), onward(near)


def named_slots(routes, experts):
    tokens, picks = routes.shape
    experts_of = iota((tokens, experts), 1)
    named = jnp.zeros((tokens, experts), F32)
    for k in range(picks):
        named = named + (routes[:, k : k + 1] == experts_of).astype(F32)
    earlier = (iota((tokens, tokens), 1) < iota((tokens, tokens), 0)).astype(BF)
    before = dot(earlier, named.astype(BF))
    return jnp.where(named > 0.5, before, -1.0)


def spread(values, experts):
    rows = experts * ROWS
    repeat = (iota((experts, rows), 1) // ROWS == iota((experts, rows), 0)).astype(BF)
    return dot(values.astype(BF), repeat)


def pack_body(
    tokens_ref, routes_ref, down_ref, out_ref, near_ref, crossed_ref,
    tokens_here, routes_here, down_here, sems,
):
    here = place_here()
    rows = out_ref.shape[0]
    experts = rows // ROWS
    steps, picks, tokens = routes_ref.shape
    part = tokens_ref.shape[2] // 8
    columns = pl.ds(pl.multiple_of((here // 2) * 2 * part, 128), 2 * part)
    fetch_routes = pltpu.make_async_copy(routes_ref, routes_here, sems.at[0])
    fetch_tokens = pltpu.make_async_copy(tokens_ref.at[:, :, columns], tokens_here, sems.at[1])
    fetch_down = pltpu.make_async_copy(down_ref, down_here, sems.at[2])
    fetch_routes.start()
    fetch_tokens.start()
    fetch_down.start()
    place = iota((rows, tokens), 0) % ROWS
    repeat = (iota((rows, experts), 0) // ROWS == iota((rows, experts), 1)).astype(BF)
    earlier = (iota((tokens, tokens), 0) < iota((tokens, tokens), 1)).astype(BF)
    experts_of = iota((experts, tokens), 0)
    fetch_routes.wait()
    slots = []
    for step in range(steps):
        named = jnp.zeros((experts, tokens), F32)
        for k in range(picks):
            named = named + (routes_here[step, k : k + 1, :] == experts_of).astype(F32)
        before = dot(named.astype(BF), earlier)
        slots.append(dot(repeat, jnp.where(named > 0.5, before, -1.0).astype(BF)))
    fetch_tokens.wait()
    main = jnp.zeros((rows, part), F32)
    for step in range(steps):
        both = tokens_here[step]
        own = jnp.where(here % 2 == 0, both[:, :part], both[:, part:])
        wanted = (place - CAP * step).astype(F32)
        chosen = ((slots[step] == wanted) & (wanted >= 0)).astype(BF)
        main = main + dot(chosen, own)
    last = dot((slots[-1] == CAP - 1.0).astype(BF), own)
    out_ref[:, :part] = main.astype(BF)
    out_ref[:, part:] = ninth_columns(last, part)
    fetch_down.wait()
    core = here % 2
    units, wide = crossed_ref.shape

    def columns(target):
        return down_here[:, pl.ds(pl.multiple_of((target // 2) * wide, 128), wide)]

    near_ref[:units, :] = columns(here ^ (4 + 2 * core))
    near_ref[units:, :] = columns(here ^ 2)
    crossed_ref[...] = columns(here ^ (7 - 2 * core))


def ninth_columns(last, part):
    row = iota((last.shape[0], HALF), 0) % ROWS
    tail = jnp.zeros((last.shape[0], HALF), F32)
    for i in range(part // HALF):
        tail = tail + jnp.where(row == i, last[:, i * HALF : (i + 1) * HALF], 0.0)
    return tail.astype(BF)


def gates_body(_, routes_ref, gates_ref, out_ref):
    steps, tokens, picks = routes_ref.shape
    rows = out_ref.shape[2]
    experts = rows // ROWS
    out_ref[...] = jnp.zeros(out_ref.shape, BF)
    place = iota((tokens, rows), 1) % ROWS
    experts_of = iota((tokens, experts), 1)
    for step in range(steps):
        routes = routes_ref[step]
        gates = gates_ref[step]
        slots = spread(named_slots(routes, experts), experts)
        gate = jnp.zeros((tokens, experts), F32)
        for k in range(picks):
            gate = gate + jnp.where(routes[:, k : k + 1] == experts_of, gates[:, k : k + 1], 0.0)
        high = gate.astype(BF)
        low = gate - high.astype(F32)
        wanted = (place - CAP * step).astype(F32)
        chosen = (slots == wanted) & (wanted >= 0)
        for n, part in enumerate((spread(high, experts), spread(low, experts))):
            out_ref[n, 16 * step : 16 * step + tokens, :] = jnp.where(chosen, part, 0.0).astype(BF)
            if step == steps - 1:
                for i in range(7):
                    start = 16 * (steps + i)
                    out_ref[n, start : start + tokens, :] = jnp.where(
                        (slots == CAP - 1.0) & (place == i), part, 0.0
                    ).astype(BF)


def other_slices_body(_, gate_ref, up_ref, other_ref):
    units = gate_ref.shape[1]
    part = gate_ref.shape[0] // 8
    for m, source in enumerate(sources(place_here() ^ 1)):
        offset = pl.multiple_of(source * part, HALF)
        rows = slice(m * part, (m + 1) * part)
        other_ref[rows, :units] = gate_ref[pl.ds(offset, part), :]
        other_ref[rows, units:] = up_ref[pl.ds(offset, part), :]


def partial_body(*refs):
    pieces, (gate_ref, up_ref, other_ref, keep_ref, send_ref) = refs[:4], refs[5:]
    rows = pieces[0].shape[0]
    experts = rows // ROWS
    part = gate_ref.shape[0] // 8
    wide = keep_ref.shape[1]
    blocks_of = sources(place_here())

    def weights(m, start, size):
        offset = pl.multiple_of(blocks_of[m] * part + start, HALF)
        return jnp.concatenate(
            [
                gate_ref[pl.ds(offset, size), :],
                up_ref[pl.ds(offset, size), :],
                other_ref[m * part + start : m * part + start + size, :],
            ],
            axis=1,
        )

    total = jnp.zeros((rows, 2 * wide), F32)
    for m in range(4):
        total = total + dot(pieces[m][:, :part], weights(m, 0, part))
    keep_ref[:rows, :] = total[:, :wide]
    send_ref[:rows, :] = total[:, wide:]
    tail = jnp.concatenate([pieces[m][:, part:] for m in range(4)], axis=1)
    blocks = part // HALF
    source = iota((blocks * experts, rows), 0)
    wanted = (source % experts) * ROWS + source // experts
    chosen = (iota((blocks * experts, rows), 1) == wanted).astype(BF)
    ninth = dot(chosen, tail).astype(BF)
    total = jnp.zeros((experts, 2 * wide), F32)
    for i in range(blocks):
        block_weights = jnp.concatenate([weights(m, i * HALF, HALF) for m in range(4)], axis=0)
        total = total + dot(ninth[i * experts : (i + 1) * experts], block_weights)
    keep_ref[rows:, :] = total[:, :wide]
    send_ref[rows:, :] = total[:, wide:]


def hidden_body(one_ref, two_ref, out_ref):
    units = out_ref.shape[1]
    gate = one_ref[:, :units] + two_ref[:, :units]
    up = one_ref[:, units:] + two_ref[:, units:]
    out_ref[...] = (gate / (1.0 + jnp.exp(-gate)) * up).astype(BF)


def down_body(own_h, near_h, crossed_h, far_h, down_ref, near_w, crossed_w, far_w, keep_ref, send_ref):
    part, units = keep_ref.shape[1], down_ref.shape[0]
    here = pl.ds(pl.multiple_of((place_here() // 2) * 2 * part, 128), 2 * part)
    total = dot(own_h[...], down_ref[:, here]) + dot(near_h[...], near_w[:units, :])
    total = total + dot(crossed_h[...], crossed_w[...]) + dot(far_h[...], far_w[...])
    first = place_here() % 2 == 0
    keep_ref[...] = jnp.where(first, total[:, :part], total[:, part:])
    send_ref[:, :part] = jnp.where(first, total[:, part:], total[:, :part]).astype(BF)
    send_ref[:, part:] = jnp.zeros((total.shape[0], HALF), BF)


def repack_body(one_ref, two_ref, out_ref):
    rows, part = out_ref.shape[0], one_ref.shape[1]
    experts = rows // ROWS
    total = (one_ref[...] + two_ref[:, :part].astype(F32)).astype(BF)
    out_ref[:, :part] = total[:rows]
    repeat = (iota((rows, experts), 0) // ROWS == iota((rows, experts), 1)).astype(BF)
    out_ref[:, part:] = ninth_columns(dot(repeat, total[rows:]), part)


def combine_body(gates_ref, rows_ref, out_ref):
    steps, tokens, part = out_ref.shape
    values = rows_ref[...]
    total = dot(gates_ref[0], values) + dot(gates_ref[1], values)
    for step in range(steps):
        out = total[16 * step : 16 * step + tokens, :part]
        if step == steps - 1:
            more = [
                total[16 * (steps + i) : 16 * (steps + i) + tokens, part:]
                for i in range(part // HALF)
            ]
            out = out + jnp.concatenate(more, axis=1)
        out_ref[step] = out.astype(BF)


def local(
    latent_cache,
    new_latent,
    queries,
    lengths,
    token_rows,
    routes,
    route_gates,
    gate_proj,
    up_proj,
    down_proj,
):
    experts = lax.axis_size("grp")
    rows = experts * ROWS
    steps, tokens, width = token_rows.shape
    part = width // 8
    units = gate_proj.shape[2]
    down_proj = down_proj.reshape(units, width)
    packed, near_down, crossed_down = pl.pallas_call(
        pack_body,
        out_shape=[
            jax.ShapeDtypeStruct((rows, part + HALF), BF),
            jax.ShapeDtypeStruct((2 * units, 2 * part), BF),
            jax.ShapeDtypeStruct((units, 2 * part), BF),
        ],
        in_specs=[HBM] * 3,
        out_specs=[VMEM] * 3,
        scratch_shapes=[
            pltpu.VMEM((steps, tokens, 2 * part), BF),
            pltpu.VMEM((steps, routes.shape[2], tokens), jnp.int32),
            pltpu.VMEM((units, width), BF),
            pltpu.SemaphoreType.DMA((3,)),
        ],
        compiler_params=pltpu.CompilerParams(vmem_limit_bytes=20 * 1024 * 1024),
        cost_estimate=pl.CostEstimate(flops=10**8, bytes_accessed=10**6, transcendentals=0),
        name="pack",
    )(token_rows, jnp.swapaxes(routes, 1, 2), down_proj)
    arrived = lax.all_to_all(
        packed.reshape(experts, ROWS, part + HALF), "grp", split_axis=0, concat_axis=0, tiled=True
    ).reshape(rows, part + HALF)

    gate_proj, up_proj = gate_proj.reshape(width, units), up_proj.reshape(width, units)
    near_down, crossed_down = to_near(near_down), to_crossed(crossed_down)
    far_down = onward(near_down[units:])
    arrived, near_down, crossed_down, far_down = lax.optimization_barrier(
        (arrived, near_down, crossed_down, far_down)
    )
    other = call(
        other_slices_body, jax.ShapeDtypeStruct((width // 2, 2 * units), BF),
        [VMEM] * 3, 10**6, 4 * 10**6, "other_slices",
    )(arrived, gate_proj, up_proj)
    other = swap(other, 1)

    keep, send = call(
        partial_body, [jax.ShapeDtypeStruct((rows + experts, 2 * units), F32)] * 2,
        [VMEM] * 4 + [HBM] + [VMEM] * 3, 10**9, 6 * 10**6, "partial",
    )(*gather(arrived), far_down, gate_proj, up_proj, other)
    hidden = call(
        hidden_body, jax.ShapeDtypeStruct((rows + experts, units), BF), [VMEM] * 2,
        10**7, 10**6, "hidden",
    )(keep, swap(send, 1))
    keep, send = call(
        down_body,
        [
            jax.ShapeDtypeStruct((rows + experts, part), F32),
            jax.ShapeDtypeStruct((rows + experts, part + HALF), BF),
        ],
        [VMEM] * 8, 10**9, 3 * 10**6, "down",
    )(*gather(hidden), down_proj, near_down, crossed_down, far_down)
    outgoing = call(
        repack_body, jax.ShapeDtypeStruct((rows, part + HALF), BF), [VMEM] * 2,
        10**8, 2 * 10**6, "repack",
    )(keep, swap(send, 1))
    returned = lax.all_to_all(
        outgoing.reshape(experts, ROWS, part + HALF), "grp", split_axis=0, concat_axis=0, tiled=True
    ).reshape(rows, part + HALF)

    heads = queries.shape[2]
    send, keep = call(
        attend_body, [jax.ShapeDtypeStruct((steps * heads, KL // 2 + 256), F32)] * 2,
        [HBM, SMEM, VMEM, VMEM, VMEM], 3 * 10**8, 2 * 10**6, "attend",
    )(
        outgoing,
        lengths,
        queries.reshape(steps * heads, queries.shape[3]),
        latent_cache[0].T,
        new_latent.reshape(steps, new_latent.shape[2]),
    )
    attention = call(
        merge_body, jax.ShapeDtypeStruct((steps * heads, KL // 2), BF), [VMEM, VMEM],
        10**6, 10**6, "merge",
    )(keep, swap(send, 4))
    gates = call(
        gates_body,
        jax.ShapeDtypeStruct((2, 16 * (steps + part // HALF), rows), BF),
        [HBM, VMEM, VMEM], 10**8, 10**6, "gates",
    )(outgoing, routes, route_gates)
    moe = call(
        combine_body, jax.ShapeDtypeStruct((steps, tokens, part), BF), [VMEM, VMEM],
        10**8, 10**6, "combine",
    )(gates, returned)
    return attention.reshape(steps, 1, heads, KL // 2), moe


def solution(mesh):
    in_specs = (
        P("grp", "sec", None),
        P(None, "grp", None),
        P(None, "grp", "tp", None),
        P("grp"),
        P(None, "grp", None),
        P(None, "grp", None),
        P(None, "grp", None),
        P("grp", None, ("sec", "tp")),
        P("grp", None, ("sec", "tp")),
        P("grp", ("sec", "tp"), None),
    )
    out_specs = (P(None, "grp", "tp", "sec"), P(None, "grp", ("sec", "tp")))
    return jax.shard_map(local, mesh=mesh, in_specs=in_specs, out_specs=out_specs, check_vma=False)
```

```python
import jax
import jax.numpy as jnp
from jax import lax
from jax.experimental import pallas as pl
from jax.experimental.pallas import tpu as pltpu
from jax.sharding import PartitionSpec as P

CAP = 3
KL = 512
ROWS = 8
HALF = 64

score_scale = 192.0 ** (-0.5)
neg_big = -1e30
BF = jnp.bfloat16
F32 = jnp.float32
LINE = ("sec", "tp")

SMEM = pl.BlockSpec(memory_space=pltpu.SMEM)
VMEM = pl.BlockSpec(memory_space=pltpu.VMEM)
HBM = pl.BlockSpec(memory_space=pltpu.HBM)


def dot(a, b, dims=((1,), (0,))):
    return lax.dot_general(a, b, (dims, ((), ())), preferred_element_type=F32)


def iota(shape, axis):
    return lax.broadcasted_iota(jnp.int32, shape, axis)


def call(body, out_shape, in_specs, flops, moved, name):
    single = not isinstance(out_shape, (list, tuple))
    return pl.pallas_call(
        body,
        out_shape=out_shape,
        in_specs=in_specs,
        out_specs=VMEM if single else [VMEM] * len(out_shape),
        compiler_params=pltpu.CompilerParams(vmem_limit_bytes=20 * 1024 * 1024),
        cost_estimate=pl.CostEstimate(flops=flops, bytes_accessed=moved, transcendentals=0),
        name=name,
    )


def attend_body(_, length_ref, q_ref, cache_ref, new_ref, send_ref, keep_ref):
    section, length = lax.axis_index("sec").astype(jnp.int32), length_ref[0]
    q = q_ref[...]
    rows, local_length = q.shape[0], cache_ref.shape[1]
    steps = new_ref.shape[0]
    heads = rows // steps
    scores = dot(q, cache_ref[...]) * score_scale
    usable = iota((rows, local_length), 1) + section * local_length < length
    scores = jnp.where(usable, scores, neg_big)
    top = jnp.max(scores, axis=1, keepdims=True)
    new_rows = new_ref[...]
    fresh = dot(q, new_rows, ((1,), (1,))) * score_scale
    step_of = iota((rows, steps), 0) // heads
    causal = (iota((rows, steps), 1) <= step_of) & (section == 0)
    fresh = jnp.where(causal, fresh, neg_big)
    top = jnp.maximum(top, jnp.max(fresh, axis=1, keepdims=True))
    weights = jnp.where(usable, jnp.exp(scores - top), 0.0)
    new_weights = jnp.where(causal, jnp.exp(fresh - top), 0.0)
    total = jnp.sum(weights, axis=1, keepdims=True) + jnp.sum(new_weights, axis=1, keepdims=True)
    out = dot(weights.astype(BF), cache_ref[:KL, :], ((1,), (1,)))
    values = new_rows[:, :KL].astype(F32)
    for t in range(steps):
        out = out + new_weights[:, t : t + 1] * values[t : t + 1, :]
    mine = section == 0
    half = KL // 2
    keep_ref[:, :half] = jnp.where(mine, out[:, :half], out[:, half:])
    send_ref[:, :half] = jnp.where(mine, out[:, half:], out[:, :half])
    for ref in (keep_ref, send_ref):
        ref[:, half : half + 128] = jnp.broadcast_to(top, (rows, 128))
        ref[:, half + 128 : half + 256] = jnp.broadcast_to(total, (rows, 128))


def merge_body(one_ref, two_ref, out_ref):
    half = out_ref.shape[1]
    top_one, top_two = one_ref[:, half : half + 1], two_ref[:, half : half + 1]
    top = jnp.maximum(top_one, top_two)
    factor_one, factor_two = jnp.exp(top_one - top), jnp.exp(top_two - top)
    total = (
        one_ref[:, half + 128 : half + 129] * factor_one
        + two_ref[:, half + 128 : half + 129] * factor_two
    )
    out = one_ref[:, :half] * factor_one + two_ref[:, :half] * factor_two
    out_ref[...] = (out / total).astype(BF)


def place_here():
    return lax.axis_index(LINE).astype(jnp.int32)


def sources(d):
    core = d % 2
    return d, d ^ (4 + 2 * core), d ^ (5 + 2 * core), d ^ 2


def permute(value, target):
    return lax.ppermute(value, LINE, [(d, target(d)) for d in range(8)])


def swap(value, k):
    return permute(value, lambda d: d ^ k)


def to_near(value):
    return permute(value, lambda d: d ^ (4 + 2 * (d % 2)))


def to_crossed(value):
    return permute(value, lambda d: d ^ (7 - 2 * (d % 2)))


def onward(value):
    return permute(value, lambda d: d ^ (6 - 2 * (d % 2)))


def gather(own):
    near = to_near(own)
    return own, near, to_crossed(own), onward(near)


def named_slots(routes, experts):
    tokens, picks = routes.shape
    experts_of = iota((tokens, experts), 1)
    named = jnp.zeros((tokens, experts), F32)
    for k in range(picks):
        named = named + (routes[:, k : k + 1] == experts_of).astype(F32)
    earlier = (iota((tokens, tokens), 1) < iota((tokens, tokens), 0)).astype(BF)
    before = dot(earlier, named.astype(BF))
    return jnp.where(named > 0.5, before, -1.0)


def spread(values, experts):
    rows = experts * ROWS
    repeat = (iota((experts, rows), 1) // ROWS == iota((experts, rows), 0)).astype(BF)
    return dot(values.astype(BF), repeat)


def pack_body(
    tokens_ref, routes_ref, down_ref, out_ref, near_ref, crossed_ref,
    tokens_here, routes_here, down_here, sems,
):
    here = place_here()
    rows = out_ref.shape[0]
    experts = rows // ROWS
    steps, picks, tokens = routes_ref.shape
    part = tokens_ref.shape[2] // 8
    columns = pl.ds(pl.multiple_of((here // 2) * 2 * part, 128), 2 * part)
    fetch_routes = pltpu.make_async_copy(routes_ref, routes_here, sems.at[0])
    fetch_tokens = pltpu.make_async_copy(tokens_ref.at[:, :, columns], tokens_here, sems.at[1])
    fetch_down = pltpu.make_async_copy(down_ref, down_here, sems.at[2])
    fetch_routes.start()
    fetch_tokens.start()
    fetch_down.start()
    place = iota((rows, tokens), 0) % ROWS
    repeat = (iota((rows, experts), 0) // ROWS == iota((rows, experts), 1)).astype(BF)
    earlier = (iota((tokens, tokens), 0) < iota((tokens, tokens), 1)).astype(BF)
    experts_of = iota((experts, tokens), 0)
    fetch_routes.wait()
    slots = []
    for step in range(steps):
        named = jnp.zeros((experts, tokens), F32)
        for k in range(picks):
            named = named + (routes_here[step, k : k + 1, :] == experts_of).astype(F32)
        before = dot(named.astype(BF), earlier)
        slots.append(dot(repeat, jnp.where(named > 0.5, before, -1.0).astype(BF)))
    fetch_tokens.wait()
    main = jnp.zeros((rows, part), F32)
    for step in range(steps):
        both = tokens_here[step]
        own = jnp.where(here % 2 == 0, both[:, :part], both[:, part:])
        wanted = (place - CAP * step).astype(F32)
        chosen = ((slots[step] == wanted) & (wanted >= 0)).astype(BF)
        main = main + dot(chosen, own)
    last = dot((slots[-1] == CAP - 1.0).astype(BF), own)
    out_ref[:, :part] = main.astype(BF)
    out_ref[:, part:] = ninth_columns(last, part)
    fetch_down.wait()
    core = here % 2
    units, wide = crossed_ref.shape

    def columns(target):
        return down_here[:, pl.ds(pl.multiple_of((target // 2) * wide, 128), wide)]

    near_ref[:units, :] = columns(here ^ (4 + 2 * core))
    near_ref[units:, :] = columns(here ^ 2)
    crossed_ref[...] = columns(here ^ (7 - 2 * core))


def ninth_columns(last, part):
    row = iota((last.shape[0], HALF), 0) % ROWS
    tail = jnp.zeros((last.shape[0], HALF), F32)
    for i in range(part // HALF):
        tail = tail + jnp.where(row == i, last[:, i * HALF : (i + 1) * HALF], 0.0)
    return tail.astype(BF)


def gates_body(_, routes_ref, gates_ref, out_ref):
    steps, tokens, picks = routes_ref.shape
    rows = out_ref.shape[2]
    experts = rows // ROWS
    out_ref[...] = jnp.zeros(out_ref.shape, BF)
    place = iota((tokens, rows), 1) % ROWS
    experts_of = iota((tokens, experts), 1)
    for step in range(steps):
        routes = routes_ref[step]
        gates = gates_ref[step]
        slots = spread(named_slots(routes, experts), experts)
        gate = jnp.zeros((tokens, experts), F32)
        for k in range(picks):
            gate = gate + jnp.where(routes[:, k : k + 1] == experts_of, gates[:, k : k + 1], 0.0)
        high = gate.astype(BF)
        low = gate - high.astype(F32)
        wanted = (place - CAP * step).astype(F32)
        chosen = (slots == wanted) & (wanted >= 0)
        for n, part in enumerate((spread(high, experts), spread(low, experts))):
            out_ref[n, 16 * step : 16 * step + tokens, :] = jnp.where(chosen, part, 0.0).astype(BF)
            if step == steps - 1:
                for i in range(7):
                    start = 16 * (steps + i)
                    out_ref[n, start : start + tokens, :] = jnp.where(
                        (slots == CAP - 1.0) & (place == i), part, 0.0
                    ).astype(BF)


def other_slices_body(_, gate_ref, up_ref, other_ref):
    units = gate_ref.shape[1]
    part = gate_ref.shape[0] // 8
    for m, source in enumerate(sources(place_here() ^ 1)):
        offset = pl.multiple_of(source * part, HALF)
        rows = slice(m * part, (m + 1) * part)
        other_ref[rows, :units] = gate_ref[pl.ds(offset, part), :]
        other_ref[rows, units:] = up_ref[pl.ds(offset, part), :]


def partial_body(*refs):
    pieces, (gate_ref, up_ref, other_ref, keep_ref, send_ref) = refs[:4], refs[5:]
    rows = pieces[0].shape[0]
    experts = rows // ROWS
    part = gate_ref.shape[0] // 8
    wide = keep_ref.shape[1]
    blocks_of = sources(place_here())

    def weights(m, start, size):
        offset = pl.multiple_of(blocks_of[m] * part + start, HALF)
        return jnp.concatenate(
            [
                gate_ref[pl.ds(offset, size), :],
                up_ref[pl.ds(offset, size), :],
                other_ref[m * part + start : m * part + start + size, :],
            ],
            axis=1,
        )

    total = jnp.zeros((rows, 2 * wide), F32)
    for m in range(4):
        total = total + dot(pieces[m][:, :part], weights(m, 0, part))
    keep_ref[:rows, :] = total[:, :wide]
    send_ref[:rows, :] = total[:, wide:]
    tail = jnp.concatenate([pieces[m][:, part:] for m in range(4)], axis=1)
    blocks = part // HALF
    source = iota((blocks * experts, rows), 0)
    wanted = (source % experts) * ROWS + source // experts
    chosen = (iota((blocks * experts, rows), 1) == wanted).astype(BF)
    ninth = dot(chosen, tail).astype(BF)
    total = jnp.zeros((experts, 2 * wide), F32)
    for i in range(blocks):
        block_weights = jnp.concatenate([weights(m, i * HALF, HALF) for m in range(4)], axis=0)
        total = total + dot(ninth[i * experts : (i + 1) * experts], block_weights)
    keep_ref[rows:, :] = total[:, :wide]
    send_ref[rows:, :] = total[:, wide:]


def hidden_body(one_ref, two_ref, out_ref):
    units = out_ref.shape[1]
    gate = one_ref[:, :units] + two_ref[:, :units]
    up = one_ref[:, units:] + two_ref[:, units:]
    out_ref[...] = (gate / (1.0 + jnp.exp(-gate)) * up).astype(BF)


def down_body(own_h, near_h, crossed_h, far_h, down_ref, near_w, crossed_w, far_w, keep_ref, send_ref):
    part, units = keep_ref.shape[1], down_ref.shape[0]
    here = pl.ds(pl.multiple_of((place_here() // 2) * 2 * part, 128), 2 * part)
    total = dot(own_h[...], down_ref[:, here]) + dot(near_h[...], near_w[:units, :])
    total = total + dot(crossed_h[...], crossed_w[...]) + dot(far_h[...], far_w[...])
    first = place_here() % 2 == 0
    keep_ref[...] = jnp.where(first, total[:, :part], total[:, part:])
    send_ref[:, :part] = jnp.where(first, total[:, part:], total[:, :part]).astype(BF)
    send_ref[:, part:] = jnp.zeros((total.shape[0], HALF), BF)


def repack_body(one_ref, two_ref, out_ref):
    rows, part = out_ref.shape[0], one_ref.shape[1]
    experts = rows // ROWS
    total = (one_ref[...] + two_ref[:, :part].astype(F32)).astype(BF)
    out_ref[:, :part] = total[:rows]
    repeat = (iota((rows, experts), 0) // ROWS == iota((rows, experts), 1)).astype(BF)
    out_ref[:, part:] = ninth_columns(dot(repeat, total[rows:]), part)


def combine_body(gates_ref, rows_ref, out_ref):
    steps, tokens, part = out_ref.shape
    values = rows_ref[...]
    total = dot(gates_ref[0], values) + dot(gates_ref[1], values)
    for step in range(steps):
        out = total[16 * step : 16 * step + tokens, :part]
        if step == steps - 1:
            more = [
                total[16 * (steps + i) : 16 * (steps + i) + tokens, part:]
                for i in range(part // HALF)
            ]
            out = out + jnp.concatenate(more, axis=1)
        out_ref[step] = out.astype(BF)


def local(
    latent_cache,
    new_latent,
    queries,
    lengths,
    token_rows,
    routes,
    route_gates,
    gate_proj,
    up_proj,
    down_proj,
):
    experts = lax.axis_size("grp")
    rows = experts * ROWS
    steps, tokens, width = token_rows.shape
    part = width // 8
    units = gate_proj.shape[2]
    down_proj = down_proj.reshape(units, width)
    packed, near_down, crossed_down = pl.pallas_call(
        pack_body,
        out_shape=[
            jax.ShapeDtypeStruct((rows, part + HALF), BF),
            jax.ShapeDtypeStruct((2 * units, 2 * part), BF),
            jax.ShapeDtypeStruct((units, 2 * part), BF),
        ],
        in_specs=[HBM] * 3,
        out_specs=[VMEM] * 3,
        scratch_shapes=[
            pltpu.VMEM((steps, tokens, 2 * part), BF),
            pltpu.VMEM((steps, routes.shape[2], tokens), jnp.int32),
            pltpu.VMEM((units, width), BF),
            pltpu.SemaphoreType.DMA((3,)),
        ],
        cost_estimate=pl.CostEstimate(flops=10**8, bytes_accessed=10**6, transcendentals=0),
        name="pack",
    )(token_rows, jnp.swapaxes(routes, 1, 2), down_proj)
    arrived = lax.all_to_all(
        packed.reshape(experts, ROWS, part + HALF), "grp", split_axis=0, concat_axis=0, tiled=True
    ).reshape(rows, part + HALF)

    gate_proj, up_proj = gate_proj.reshape(width, units), up_proj.reshape(width, units)
    near_down, crossed_down = to_near(near_down), to_crossed(crossed_down)
    arrived, near_down, crossed_down = lax.optimization_barrier(
        (arrived, near_down, crossed_down)
    )
    far_down = onward(near_down[units:])
    other = call(
        other_slices_body, jax.ShapeDtypeStruct((width // 2, 2 * units), BF),
        [VMEM] * 3, 10**6, 4 * 10**6, "other_slices",
    )(arrived, gate_proj, up_proj)
    other = swap(other, 1)

    keep, send = call(
        partial_body, [jax.ShapeDtypeStruct((rows + experts, 2 * units), F32)] * 2,
        [VMEM] * 4 + [HBM] + [VMEM] * 3, 10**9, 6 * 10**6, "partial",
    )(*gather(arrived), far_down, gate_proj, up_proj, other)
    hidden = call(
        hidden_body, jax.ShapeDtypeStruct((rows + experts, units), BF), [VMEM] * 2,
        10**7, 10**6, "hidden",
    )(keep, swap(send, 1))
    keep, send = call(
        down_body,
        [
            jax.ShapeDtypeStruct((rows + experts, part), F32),
            jax.ShapeDtypeStruct((rows + experts, part + HALF), BF),
        ],
        [VMEM] * 8, 10**9, 3 * 10**6, "down",
    )(*gather(hidden), down_proj, near_down, crossed_down, far_down)
    outgoing = call(
        repack_body, jax.ShapeDtypeStruct((rows, part + HALF), BF), [VMEM] * 2,
        10**8, 2 * 10**6, "repack",
    )(keep, swap(send, 1))
    returned = lax.all_to_all(
        outgoing.reshape(experts, ROWS, part + HALF), "grp", split_axis=0, concat_axis=0, tiled=True
    ).reshape(rows, part + HALF)

    heads = queries.shape[2]
    send, keep = call(
        attend_body, [jax.ShapeDtypeStruct((steps * heads, KL // 2 + 256), F32)] * 2,
        [HBM, SMEM, VMEM, VMEM, VMEM], 3 * 10**8, 2 * 10**6, "attend",
    )(
        outgoing,
        lengths,
        queries.reshape(steps * heads, queries.shape[3]),
        latent_cache[0].T,
        new_latent.reshape(steps, new_latent.shape[2]),
    )
    attention = call(
        merge_body, jax.ShapeDtypeStruct((steps * heads, KL // 2), BF), [VMEM, VMEM],
        10**6, 10**6, "merge",
    )(keep, swap(send, 4))
    gates = call(
        gates_body,
        jax.ShapeDtypeStruct((2, 16 * (steps + part // HALF), rows), BF),
        [HBM, VMEM, VMEM], 10**8, 10**6, "gates",
    )(outgoing, routes, route_gates)
    moe = call(
        combine_body, jax.ShapeDtypeStruct((steps, tokens, part), BF), [VMEM, VMEM],
        10**8, 10**6, "combine",
    )(gates, returned)
    return attention.reshape(steps, 1, heads, KL // 2), moe


def solution(mesh):
    in_specs = (
        P("grp", "sec", None),
        P(None, "grp", None),
        P(None, "grp", "tp", None),
        P("grp"),
        P(None, "grp", None),
        P(None, "grp", None),
        P(None, "grp", None),
        P("grp", None, ("sec", "tp")),
        P("grp", None, ("sec", "tp")),
        P("grp", ("sec", "tp"), None),
    )
    out_specs = (P(None, "grp", "tp", "sec"), P(None, "grp", ("sec", "tp")))
    return jax.shard_map(local, mesh=mesh, in_specs=in_specs, out_specs=out_specs, check_vma=False)
```

```python
import jax
import jax.numpy as jnp
from jax import lax
from jax.experimental import pallas as pl
from jax.experimental.pallas import tpu as pltpu
from jax.sharding import PartitionSpec as P

CAP = 3
KL = 512
ROWS = 8
HALF = 64

score_scale = 192.0 ** (-0.5)
neg_big = -1e30
BF = jnp.bfloat16
F32 = jnp.float32
LINE = ("sec", "tp")

SMEM = pl.BlockSpec(memory_space=pltpu.SMEM)
VMEM = pl.BlockSpec(memory_space=pltpu.VMEM)
HBM = pl.BlockSpec(memory_space=pltpu.HBM)


def dot(a, b, dims=((1,), (0,))):
    return lax.dot_general(a, b, (dims, ((), ())), preferred_element_type=F32)


def iota(shape, axis):
    return lax.broadcasted_iota(jnp.int32, shape, axis)


def call(body, out_shape, in_specs, flops, moved, name):
    single = not isinstance(out_shape, (list, tuple))
    return pl.pallas_call(
        body,
        out_shape=out_shape,
        in_specs=in_specs,
        out_specs=VMEM if single else [VMEM] * len(out_shape),
        compiler_params=pltpu.CompilerParams(vmem_limit_bytes=20 * 1024 * 1024),
        cost_estimate=pl.CostEstimate(flops=flops, bytes_accessed=moved, transcendentals=0),
        name=name,
    )


def attend_body(_, length_ref, q_ref, cache_ref, new_ref, send_ref, keep_ref):
    section, length = lax.axis_index("sec").astype(jnp.int32), length_ref[0]
    q = q_ref[...]
    rows, local_length = q.shape[0], cache_ref.shape[1]
    steps = new_ref.shape[0]
    heads = rows // steps
    scores = dot(q, cache_ref[...]) * score_scale
    usable = iota((rows, local_length), 1) + section * local_length < length
    scores = jnp.where(usable, scores, neg_big)
    top = jnp.max(scores, axis=1, keepdims=True)
    new_rows = new_ref[...]
    fresh = dot(q, new_rows, ((1,), (1,))) * score_scale
    step_of = iota((rows, steps), 0) // heads
    causal = (iota((rows, steps), 1) <= step_of) & (section == 0)
    fresh = jnp.where(causal, fresh, neg_big)
    top = jnp.maximum(top, jnp.max(fresh, axis=1, keepdims=True))
    weights = jnp.where(usable, jnp.exp(scores - top), 0.0)
    new_weights = jnp.where(causal, jnp.exp(fresh - top), 0.0)
    total = jnp.sum(weights, axis=1, keepdims=True) + jnp.sum(new_weights, axis=1, keepdims=True)
    out = dot(weights.astype(BF), cache_ref[:KL, :], ((1,), (1,)))
    values = new_rows[:, :KL].astype(F32)
    for t in range(steps):
        out = out + new_weights[:, t : t + 1] * values[t : t + 1, :]
    mine = section == 0
    half = KL // 2
    keep_ref[:, :half] = jnp.where(mine, out[:, :half], out[:, half:])
    send_ref[:, :half] = jnp.where(mine, out[:, half:], out[:, :half])
    for ref in (keep_ref, send_ref):
        ref[:, half : half + 128] = jnp.broadcast_to(top, (rows, 128))
        ref[:, half + 128 : half + 256] = jnp.broadcast_to(total, (rows, 128))


def merge_body(one_ref, two_ref, out_ref):
    half = out_ref.shape[1]
    top_one, top_two = one_ref[:, half : half + 1], two_ref[:, half : half + 1]
    top = jnp.maximum(top_one, top_two)
    factor_one, factor_two = jnp.exp(top_one - top), jnp.exp(top_two - top)
    total = (
        one_ref[:, half + 128 : half + 129] * factor_one
        + two_ref[:, half + 128 : half + 129] * factor_two
    )
    out = one_ref[:, :half] * factor_one + two_ref[:, :half] * factor_two
    out_ref[...] = (out / total).astype(BF)


def place_here():
    return lax.axis_index(LINE).astype(jnp.int32)


def sources(d):
    core = d % 2
    return d, d ^ (4 + 2 * core), d ^ (5 + 2 * core), d ^ 2


def permute(value, target):
    return lax.ppermute(value, LINE, [(d, target(d)) for d in range(8)])


def swap(value, k):
    return permute(value, lambda d: d ^ k)


def to_near(value):
    return permute(value, lambda d: d ^ (4 + 2 * (d % 2)))


def to_crossed(value):
    return permute(value, lambda d: d ^ (7 - 2 * (d % 2)))


def onward(value):
    return permute(value, lambda d: d ^ (6 - 2 * (d % 2)))


def gather(own):
    near = to_near(own)
    return own, near, to_crossed(own), onward(near)


def named_slots(routes, experts):
    tokens, picks = routes.shape
    experts_of = iota((tokens, experts), 1)
    named = jnp.zeros((tokens, experts), F32)
    for k in range(picks):
        named = named + (routes[:, k : k + 1] == experts_of).astype(F32)
    earlier = (iota((tokens, tokens), 1) < iota((tokens, tokens), 0)).astype(BF)
    before = dot(earlier, named.astype(BF))
    return jnp.where(named > 0.5, before, -1.0)


def spread(values, experts):
    rows = experts * ROWS
    repeat = (iota((experts, rows), 1) // ROWS == iota((experts, rows), 0)).astype(BF)
    return dot(values.astype(BF), repeat)


def pack_body(
    tokens_ref, routes_ref, down_ref, out_ref, near_ref, crossed_ref,
    tokens_here, routes_here, down_here, sems,
):
    here = place_here()
    rows = out_ref.shape[0]
    experts = rows // ROWS
    steps, picks, tokens = routes_ref.shape
    part = tokens_ref.shape[2] // 8
    columns = pl.ds(pl.multiple_of((here // 2) * 2 * part, 128), 2 * part)
    fetch_routes = pltpu.make_async_copy(routes_ref, routes_here, sems.at[0])
    fetch_tokens = pltpu.make_async_copy(tokens_ref.at[:, :, columns], tokens_here, sems.at[1])
    fetch_down = pltpu.make_async_copy(down_ref, down_here, sems.at[2])
    fetch_routes.start()
    fetch_tokens.start()
    fetch_down.start()
    place = iota((rows, tokens), 0) % ROWS
    repeat = (iota((rows, experts), 0) // ROWS == iota((rows, experts), 1)).astype(BF)
    earlier = (iota((tokens, tokens), 0) < iota((tokens, tokens), 1)).astype(BF)
    experts_of = iota((experts, tokens), 0)
    fetch_routes.wait()
    slots = []
    for step in range(steps):
        named = jnp.zeros((experts, tokens), F32)
        for k in range(picks):
            named = named + (routes_here[step, k : k + 1, :] == experts_of).astype(F32)
        before = dot(named.astype(BF), earlier)
        slots.append(dot(repeat, jnp.where(named > 0.5, before, -1.0).astype(BF)))
    fetch_tokens.wait()
    main = jnp.zeros((rows, part), F32)
    for step in range(steps):
        both = tokens_here[step]
        own = jnp.where(here % 2 == 0, both[:, :part], both[:, part:])
        wanted = (place - CAP * step).astype(F32)
        chosen = ((slots[step] == wanted) & (wanted >= 0)).astype(BF)
        main = main + dot(chosen, own)
    last = dot((slots[-1] == CAP - 1.0).astype(BF), own)
    out_ref[:, :part] = main.astype(BF)
    out_ref[:, part:] = ninth_columns(last, part)
    fetch_down.wait()
    core = here % 2
    units, wide = crossed_ref.shape

    def columns(target):
        return down_here[:, pl.ds(pl.multiple_of((target // 2) * wide, 128), wide)]

    near_ref[:units, :] = columns(here ^ (4 + 2 * core))
    near_ref[units:, :] = columns(here ^ 2)
    crossed_ref[...] = columns(here ^ (7 - 2 * core))


def ninth_columns(last, part):
    row = iota((last.shape[0], HALF), 0) % ROWS
    tail = jnp.zeros((last.shape[0], HALF), F32)
    for i in range(part // HALF):
        tail = tail + jnp.where(row == i, last[:, i * HALF : (i + 1) * HALF], 0.0)
    return tail.astype(BF)


def gates_body(_, routes_ref, gates_ref, out_ref):
    steps, tokens, picks = routes_ref.shape
    rows = out_ref.shape[2]
    experts = rows // ROWS
    out_ref[...] = jnp.zeros(out_ref.shape, BF)
    place = iota((tokens, rows), 1) % ROWS
    experts_of = iota((tokens, experts), 1)
    for step in range(steps):
        routes = routes_ref[step]
        gates = gates_ref[step]
        slots = spread(named_slots(routes, experts), experts)
        gate = jnp.zeros((tokens, experts), F32)
        for k in range(picks):
            gate = gate + jnp.where(routes[:, k : k + 1] == experts_of, gates[:, k : k + 1], 0.0)
        high = gate.astype(BF)
        low = gate - high.astype(F32)
        wanted = (place - CAP * step).astype(F32)
        chosen = (slots == wanted) & (wanted >= 0)
        for n, part in enumerate((spread(high, experts), spread(low, experts))):
            out_ref[n, 16 * step : 16 * step + tokens, :] = jnp.where(chosen, part, 0.0).astype(BF)
            if step == steps - 1:
                for i in range(7):
                    start = 16 * (steps + i)
                    out_ref[n, start : start + tokens, :] = jnp.where(
                        (slots == CAP - 1.0) & (place == i), part, 0.0
                    ).astype(BF)


def other_slices_body(_, gate_ref, up_ref, other_ref):
    units = gate_ref.shape[1]
    part = gate_ref.shape[0] // 8
    for m, source in enumerate(sources(place_here() ^ 1)):
        offset = pl.multiple_of(source * part, HALF)
        rows = slice(m * part, (m + 1) * part)
        other_ref[rows, :units] = gate_ref[pl.ds(offset, part), :]
        other_ref[rows, units:] = up_ref[pl.ds(offset, part), :]


def partial_sums(pieces, weights, out_ref):
    rows, wide = pieces[0].shape[0], out_ref.shape[1]
    experts = rows // ROWS
    part = pieces[0].shape[1] - HALF
    total = jnp.zeros((rows, wide), F32)
    for m in range(4):
        total = total + dot(pieces[m][:, :part], weights(m, 0, part))
    out_ref[:rows, :] = total
    tail = jnp.concatenate([pieces[m][:, part:] for m in range(4)], axis=1)
    blocks = part // HALF
    source = iota((blocks * experts, rows), 0)
    wanted = (source % experts) * ROWS + source // experts
    chosen = (iota((blocks * experts, rows), 1) == wanted).astype(BF)
    ninth = dot(chosen, tail).astype(BF)
    total = jnp.zeros((experts, wide), F32)
    for i in range(blocks):
        block_weights = jnp.concatenate([weights(m, i * HALF, HALF) for m in range(4)], axis=0)
        total = total + dot(ninth[i * experts : (i + 1) * experts], block_weights)
    out_ref[rows:, :] = total


def partial_send_body(*refs):
    pieces, (other_ref, out_ref) = refs[:4], refs[5:]
    part = pieces[0].shape[1] - HALF

    def weights(m, start, size):
        return other_ref[m * part + start : m * part + start + size, :]

    partial_sums(pieces, weights, out_ref)


def partial_keep_body(*refs):
    pieces, (gate_ref, up_ref, out_ref) = refs[:4], refs[4:]
    part = pieces[0].shape[1] - HALF
    blocks_of = sources(place_here())

    def weights(m, start, size):
        offset = pl.multiple_of(blocks_of[m] * part + start, HALF)
        return jnp.concatenate(
            [gate_ref[pl.ds(offset, size), :], up_ref[pl.ds(offset, size), :]], axis=1
        )

    partial_sums(pieces, weights, out_ref)


def hidden_body(one_ref, two_ref, out_ref):
    units = out_ref.shape[1]
    gate = one_ref[:, :units] + two_ref[:, :units]
    up = one_ref[:, units:] + two_ref[:, units:]
    out_ref[...] = (gate / (1.0 + jnp.exp(-gate)) * up).astype(BF)


def down_sums(core, hidden, down_ref, near_w, crossed_w, far_w, part):
    own_h, near_h, crossed_h, far_h = hidden
    units = down_ref.shape[0]

    def half(both):
        return jnp.where(core == 0, both[:, :part], both[:, part:])

    here = pl.ds(pl.multiple_of((place_here() // 2) * 2 * part, 128), 2 * part)
    total = dot(own_h[...], half(down_ref[:, here])) + dot(near_h[...], half(near_w[:units, :]))
    return total + dot(crossed_h[...], half(crossed_w[...])) + dot(far_h[...], half(far_w[...]))


def down_send_body(*refs):
    hidden, (down_ref, near_w, crossed_w, far_w, out_ref) = refs[:4], refs[4:]
    part = near_w.shape[1] // 2
    core = 1 - place_here() % 2
    total = down_sums(core, hidden, down_ref, near_w, crossed_w, far_w, part)
    out_ref[:, :part] = total.astype(BF)
    out_ref[:, part:] = jnp.zeros((total.shape[0], HALF), BF)


def down_keep_body(*refs):
    hidden, (down_ref, near_w, crossed_w, far_w, out_ref) = refs[:4], refs[4:]
    part = near_w.shape[1] // 2
    core = place_here() % 2
    out_ref[...] = down_sums(core, hidden, down_ref, near_w, crossed_w, far_w, part)


def repack_body(one_ref, two_ref, out_ref):
    rows, part = out_ref.shape[0], one_ref.shape[1]
    experts = rows // ROWS
    total = (one_ref[...] + two_ref[:, :part].astype(F32)).astype(BF)
    out_ref[:, :part] = total[:rows]
    repeat = (iota((rows, experts), 0) // ROWS == iota((rows, experts), 1)).astype(BF)
    out_ref[:, part:] = ninth_columns(dot(repeat, total[rows:]), part)


def combine_body(gates_ref, rows_ref, out_ref):
    steps, tokens, part = out_ref.shape
    values = rows_ref[...]
    total = dot(gates_ref[0], values) + dot(gates_ref[1], values)
    for step in range(steps):
        out = total[16 * step : 16 * step + tokens, :part]
        if step == steps - 1:
            more = [
                total[16 * (steps + i) : 16 * (steps + i) + tokens, part:]
                for i in range(part // HALF)
            ]
            out = out + jnp.concatenate(more, axis=1)
        out_ref[step] = out.astype(BF)


def local(
    latent_cache,
    new_latent,
    queries,
    lengths,
    token_rows,
    routes,
    route_gates,
    gate_proj,
    up_proj,
    down_proj,
):
    experts = lax.axis_size("grp")
    rows = experts * ROWS
    steps, tokens, width = token_rows.shape
    part = width // 8
    units = gate_proj.shape[2]
    down_proj = down_proj.reshape(units, width)
    packed, near_down, crossed_down = pl.pallas_call(
        pack_body,
        out_shape=[
            jax.ShapeDtypeStruct((rows, part + HALF), BF),
            jax.ShapeDtypeStruct((2 * units, 2 * part), BF),
            jax.ShapeDtypeStruct((units, 2 * part), BF),
        ],
        in_specs=[HBM] * 3,
        out_specs=[VMEM] * 3,
        scratch_shapes=[
            pltpu.VMEM((steps, tokens, 2 * part), BF),
            pltpu.VMEM((steps, routes.shape[2], tokens), jnp.int32),
            pltpu.VMEM((units, width), BF),
            pltpu.SemaphoreType.DMA((3,)),
        ],
        cost_estimate=pl.CostEstimate(flops=10**8, bytes_accessed=10**6, transcendentals=0),
        name="pack",
    )(token_rows, jnp.swapaxes(routes, 1, 2), down_proj)
    arrived = lax.all_to_all(
        packed.reshape(experts, ROWS, part + HALF), "grp", split_axis=0, concat_axis=0, tiled=True
    ).reshape(rows, part + HALF)

    gate_proj, up_proj = gate_proj.reshape(width, units), up_proj.reshape(width, units)
    near_down, crossed_down = to_near(near_down), to_crossed(crossed_down)
    arrived, near_down, crossed_down = lax.optimization_barrier(
        (arrived, near_down, crossed_down)
    )
    far_down = onward(near_down[units:])
    other = call(
        other_slices_body, jax.ShapeDtypeStruct((width // 2, 2 * units), BF),
        [VMEM] * 3, 10**6, 4 * 10**6, "other_slices",
    )(arrived, gate_proj, up_proj)
    other = swap(other, 1)

    pieces = gather(arrived)
    sums = jax.ShapeDtypeStruct((rows + experts, 2 * units), F32)
    send = call(
        partial_send_body, sums, [VMEM] * 4 + [HBM, VMEM], 10**9, 4 * 10**6, "partial_send",
    )(*pieces, far_down, other)
    keep = call(
        partial_keep_body, sums, [VMEM] * 6, 10**9, 4 * 10**6, "partial_keep",
    )(*pieces, gate_proj, up_proj)
    hidden = call(
        hidden_body, jax.ShapeDtypeStruct((rows + experts, units), BF), [VMEM] * 2,
        10**7, 10**6, "hidden",
    )(keep, swap(send, 1))
    operands = *gather(hidden), down_proj, near_down, crossed_down, far_down
    send = call(
        down_send_body, jax.ShapeDtypeStruct((rows + experts, part + HALF), BF), [VMEM] * 8,
        10**9, 2 * 10**6, "down_send",
    )(*operands)
    keep = call(
        down_keep_body, jax.ShapeDtypeStruct((rows + experts, part), F32), [VMEM] * 8,
        10**9, 2 * 10**6, "down_keep",
    )(*operands)
    outgoing = call(
        repack_body, jax.ShapeDtypeStruct((rows, part + HALF), BF), [VMEM] * 2,
        10**8, 2 * 10**6, "repack",
    )(keep, swap(send, 1))
    returned = lax.all_to_all(
        outgoing.reshape(experts, ROWS, part + HALF), "grp", split_axis=0, concat_axis=0, tiled=True
    ).reshape(rows, part + HALF)

    heads = queries.shape[2]
    send, keep = call(
        attend_body, [jax.ShapeDtypeStruct((steps * heads, KL // 2 + 256), F32)] * 2,
        [HBM, SMEM, VMEM, VMEM, VMEM], 3 * 10**8, 2 * 10**6, "attend",
    )(
        outgoing,
        lengths,
        queries.reshape(steps * heads, queries.shape[3]),
        latent_cache[0].T,
        new_latent.reshape(steps, new_latent.shape[2]),
    )
    attention = call(
        merge_body, jax.ShapeDtypeStruct((steps * heads, KL // 2), BF), [VMEM, VMEM],
        10**6, 10**6, "merge",
    )(keep, swap(send, 4))
    gates = call(
        gates_body,
        jax.ShapeDtypeStruct((2, 16 * (steps + part // HALF), rows), BF),
        [HBM, VMEM, VMEM], 10**8, 10**6, "gates",
    )(outgoing, routes, route_gates)
    moe = call(
        combine_body, jax.ShapeDtypeStruct((steps, tokens, part), BF), [VMEM, VMEM],
        10**8, 10**6, "combine",
    )(gates, returned)
    return attention.reshape(steps, 1, heads, KL // 2), moe


def solution(mesh):
    in_specs = (
        P("grp", "sec", None),
        P(None, "grp", None),
        P(None, "grp", "tp", None),
        P("grp"),
        P(None, "grp", None),
        P(None, "grp", None),
        P(None, "grp", None),
        P("grp", None, ("sec", "tp")),
        P("grp", None, ("sec", "tp")),
        P("grp", ("sec", "tp"), None),
    )
    out_specs = (P(None, "grp", "tp", "sec"), P(None, "grp", ("sec", "tp")))
    return jax.shard_map(local, mesh=mesh, in_specs=in_specs, out_specs=out_specs, check_vma=False)
```

```python
import jax
import jax.numpy as jnp
from jax import lax
from jax.experimental import pallas as pl
from jax.experimental.pallas import tpu as pltpu
from jax.sharding import PartitionSpec as P

CAP = 3
KL = 512
ROWS = 8
HALF = 64

score_scale = 192.0 ** (-0.5)
neg_big = -1e30
BF = jnp.bfloat16
F32 = jnp.float32
LINE = ("sec", "tp")

SMEM = pl.BlockSpec(memory_space=pltpu.SMEM)
VMEM = pl.BlockSpec(memory_space=pltpu.VMEM)
HBM = pl.BlockSpec(memory_space=pltpu.HBM)


def dot(a, b, dims=((1,), (0,))):
    return lax.dot_general(a, b, (dims, ((), ())), preferred_element_type=F32)


def iota(shape, axis):
    return lax.broadcasted_iota(jnp.int32, shape, axis)


def call(body, out_shape, in_specs, flops, moved, name):
    single = not isinstance(out_shape, (list, tuple))
    return pl.pallas_call(
        body,
        out_shape=out_shape,
        in_specs=in_specs,
        out_specs=VMEM if single else [VMEM] * len(out_shape),
        compiler_params=pltpu.CompilerParams(vmem_limit_bytes=20 * 1024 * 1024),
        cost_estimate=pl.CostEstimate(flops=flops, bytes_accessed=moved, transcendentals=0),
        name=name,
    )


def attend_body(_, length_ref, q_ref, cache_ref, new_ref, send_ref, keep_ref):
    section, length = lax.axis_index("sec").astype(jnp.int32), length_ref[0]
    q = q_ref[...]
    rows, local_length = q.shape[0], cache_ref.shape[1]
    steps = new_ref.shape[0]
    heads = rows // steps
    scores = dot(q, cache_ref[...]) * score_scale
    usable = iota((rows, local_length), 1) + section * local_length < length
    scores = jnp.where(usable, scores, neg_big)
    top = jnp.max(scores, axis=1, keepdims=True)
    new_rows = new_ref[...]
    fresh = dot(q, new_rows, ((1,), (1,))) * score_scale
    step_of = iota((rows, steps), 0) // heads
    causal = (iota((rows, steps), 1) <= step_of) & (section == 0)
    fresh = jnp.where(causal, fresh, neg_big)
    top = jnp.maximum(top, jnp.max(fresh, axis=1, keepdims=True))
    weights = jnp.where(usable, jnp.exp(scores - top), 0.0)
    new_weights = jnp.where(causal, jnp.exp(fresh - top), 0.0)
    total = jnp.sum(weights, axis=1, keepdims=True) + jnp.sum(new_weights, axis=1, keepdims=True)
    out = dot(weights.astype(BF), cache_ref[:KL, :], ((1,), (1,)))
    values = new_rows[:, :KL].astype(F32)
    for t in range(steps):
        out = out + new_weights[:, t : t + 1] * values[t : t + 1, :]
    mine = section == 0
    half = KL // 2
    keep_ref[:, :half] = jnp.where(mine, out[:, :half], out[:, half:])
    send_ref[:, :half] = jnp.where(mine, out[:, half:], out[:, :half])
    for ref in (keep_ref, send_ref):
        ref[:, half : half + 128] = jnp.broadcast_to(top, (rows, 128))
        ref[:, half + 128 : half + 256] = jnp.broadcast_to(total, (rows, 128))


def merge_body(one_ref, two_ref, out_ref):
    half = out_ref.shape[1]
    top_one, top_two = one_ref[:, half : half + 1], two_ref[:, half : half + 1]
    top = jnp.maximum(top_one, top_two)
    factor_one, factor_two = jnp.exp(top_one - top), jnp.exp(top_two - top)
    total = (
        one_ref[:, half + 128 : half + 129] * factor_one
        + two_ref[:, half + 128 : half + 129] * factor_two
    )
    out = one_ref[:, :half] * factor_one + two_ref[:, :half] * factor_two
    out_ref[...] = (out / total).astype(BF)


def place_here():
    return lax.axis_index(LINE).astype(jnp.int32)


def sources(d):
    core = d % 2
    return d, d ^ (4 + 2 * core), d ^ (5 + 2 * core), d ^ 2


def permute(value, target):
    return lax.ppermute(value, LINE, [(d, target(d)) for d in range(8)])


def swap(value, k):
    return permute(value, lambda d: d ^ k)


def to_near(value):
    return permute(value, lambda d: d ^ (4 + 2 * (d % 2)))


def to_crossed(value):
    return permute(value, lambda d: d ^ (7 - 2 * (d % 2)))


def onward(value):
    return permute(value, lambda d: d ^ (6 - 2 * (d % 2)))


def gather(own):
    near = to_near(own)
    return own, near, to_crossed(own), onward(near)


def named_slots(routes, experts):
    tokens, picks = routes.shape
    experts_of = iota((tokens, experts), 1)
    named = jnp.zeros((tokens, experts), F32)
    for k in range(picks):
        named = named + (routes[:, k : k + 1] == experts_of).astype(F32)
    earlier = (iota((tokens, tokens), 1) < iota((tokens, tokens), 0)).astype(BF)
    before = dot(earlier, named.astype(BF))
    return jnp.where(named > 0.5, before, -1.0)


def spread(values, experts):
    rows = experts * ROWS
    repeat = (iota((experts, rows), 1) // ROWS == iota((experts, rows), 0)).astype(BF)
    return dot(values.astype(BF), repeat)


def pack_body(
    tokens_ref, routes_ref, down_ref, out_ref, near_ref, crossed_ref,
    tokens_here, routes_here, down_here, sems,
):
    here = place_here()
    rows = out_ref.shape[0]
    experts = rows // ROWS
    steps, picks, tokens = routes_ref.shape
    part = tokens_ref.shape[2] // 8
    columns = pl.ds(pl.multiple_of((here // 2) * 2 * part, 128), 2 * part)
    fetch_routes = pltpu.make_async_copy(routes_ref, routes_here, sems.at[0])
    fetch_tokens = pltpu.make_async_copy(tokens_ref.at[:, :, columns], tokens_here, sems.at[1])
    fetch_down = pltpu.make_async_copy(down_ref, down_here, sems.at[2])
    fetch_routes.start()
    fetch_tokens.start()
    fetch_down.start()
    place = iota((rows, tokens), 0) % ROWS
    repeat = (iota((rows, experts), 0) // ROWS == iota((rows, experts), 1)).astype(BF)
    earlier = (iota((tokens, tokens), 0) < iota((tokens, tokens), 1)).astype(BF)
    experts_of = iota((experts, tokens), 0)
    fetch_routes.wait()
    slots = []
    for step in range(steps):
        named = jnp.zeros((experts, tokens), F32)
        for k in range(picks):
            named = named + (routes_here[step, k : k + 1, :] == experts_of).astype(F32)
        before = dot(named.astype(BF), earlier)
        slots.append(dot(repeat, jnp.where(named > 0.5, before, -1.0).astype(BF)))
    fetch_tokens.wait()
    main = jnp.zeros((rows, part), F32)
    for step in range(steps):
        both = tokens_here[step]
        own = jnp.where(here % 2 == 0, both[:, :part], both[:, part:])
        wanted = (place - CAP * step).astype(F32)
        chosen = ((slots[step] == wanted) & (wanted >= 0)).astype(BF)
        main = main + dot(chosen, own)
    last = dot((slots[-1] == CAP - 1.0).astype(BF), own)
    out_ref[:, :part] = main.astype(BF)
    out_ref[:, part:] = ninth_columns(last, part)
    fetch_down.wait()
    core = here % 2
    units, wide = crossed_ref.shape

    def columns(target):
        return down_here[:, pl.ds(pl.multiple_of((target // 2) * wide, 128), wide)]

    near_ref[:units, :] = columns(here ^ (4 + 2 * core))
    near_ref[units:, :] = columns(here ^ 2)
    crossed_ref[...] = columns(here ^ (7 - 2 * core))


def ninth_columns(last, part):
    row = iota((last.shape[0], HALF), 0) % ROWS
    tail = jnp.zeros((last.shape[0], HALF), F32)
    for i in range(part // HALF):
        tail = tail + jnp.where(row == i, last[:, i * HALF : (i + 1) * HALF], 0.0)
    return tail.astype(BF)


def gates_body(_, routes_ref, gates_ref, out_ref):
    steps, tokens, picks = routes_ref.shape
    rows = out_ref.shape[2]
    experts = rows // ROWS
    out_ref[...] = jnp.zeros(out_ref.shape, BF)
    place = iota((tokens, rows), 1) % ROWS
    experts_of = iota((tokens, experts), 1)
    for step in range(steps):
        routes = routes_ref[step]
        gates = gates_ref[step]
        slots = spread(named_slots(routes, experts), experts)
        gate = jnp.zeros((tokens, experts), F32)
        for k in range(picks):
            gate = gate + jnp.where(routes[:, k : k + 1] == experts_of, gates[:, k : k + 1], 0.0)
        high = gate.astype(BF)
        low = gate - high.astype(F32)
        wanted = (place - CAP * step).astype(F32)
        chosen = (slots == wanted) & (wanted >= 0)
        for n, part in enumerate((spread(high, experts), spread(low, experts))):
            out_ref[n, 16 * step : 16 * step + tokens, :] = jnp.where(chosen, part, 0.0).astype(BF)
            if step == steps - 1:
                for i in range(7):
                    start = 16 * (steps + i)
                    out_ref[n, start : start + tokens, :] = jnp.where(
                        (slots == CAP - 1.0) & (place == i), part, 0.0
                    ).astype(BF)


def other_slices_body(_, gate_ref, up_ref, other_ref):
    units = gate_ref.shape[1]
    part = gate_ref.shape[0] // 8
    for m, source in enumerate(sources(place_here() ^ 1)):
        offset = pl.multiple_of(source * part, HALF)
        rows = slice(m * part, (m + 1) * part)
        other_ref[rows, :units] = gate_ref[pl.ds(offset, part), :]
        other_ref[rows, units:] = up_ref[pl.ds(offset, part), :]


def partial_sums(pieces, weights, out_ref):
    rows, wide = pieces[0].shape[0], out_ref.shape[1]
    experts = rows // ROWS
    part = pieces[0].shape[1] - HALF
    total = jnp.zeros((rows, wide), F32)
    for m in range(4):
        total = total + dot(pieces[m][:, :part], weights(m, 0, part))
    out_ref[:rows, :] = total.astype(out_ref.dtype)
    tail = jnp.concatenate([pieces[m][:, part:] for m in range(4)], axis=1)
    blocks = part // HALF
    source = iota((blocks * experts, rows), 0)
    wanted = (source % experts) * ROWS + source // experts
    chosen = (iota((blocks * experts, rows), 1) == wanted).astype(BF)
    ninth = dot(chosen, tail).astype(BF)
    total = jnp.zeros((experts, wide), F32)
    for i in range(blocks):
        block_weights = jnp.concatenate([weights(m, i * HALF, HALF) for m in range(4)], axis=0)
        total = total + dot(ninth[i * experts : (i + 1) * experts], block_weights)
    out_ref[rows:, :] = total.astype(out_ref.dtype)


def partial_send_body(*refs):
    pieces, (other_ref, out_ref) = refs[:4], refs[5:]
    part = pieces[0].shape[1] - HALF

    def weights(m, start, size):
        return other_ref[m * part + start : m * part + start + size, :]

    partial_sums(pieces, weights, out_ref)


def partial_keep_body(*refs):
    pieces, (gate_ref, up_ref, out_ref) = refs[:4], refs[4:]
    part = pieces[0].shape[1] - HALF
    blocks_of = sources(place_here())

    def weights(m, start, size):
        offset = pl.multiple_of(blocks_of[m] * part + start, HALF)
        return jnp.concatenate(
            [gate_ref[pl.ds(offset, size), :], up_ref[pl.ds(offset, size), :]], axis=1
        )

    partial_sums(pieces, weights, out_ref)


def hidden_body(one_ref, two_ref, out_ref):
    units = out_ref.shape[1]
    gate = one_ref[:, :units] + two_ref[:, :units].astype(F32)
    up = one_ref[:, units:] + two_ref[:, units:].astype(F32)
    out_ref[...] = (gate / (1.0 + jnp.exp(-gate)) * up).astype(BF)


def down_sums(core, hidden, down_ref, near_w, crossed_w, far_w, part):
    own_h, near_h, crossed_h, far_h = hidden
    units = down_ref.shape[0]

    def half(both):
        return jnp.where(core == 0, both[:, :part], both[:, part:])

    here = pl.ds(pl.multiple_of((place_here() // 2) * 2 * part, 128), 2 * part)
    total = dot(own_h[...], half(down_ref[:, here])) + dot(near_h[...], half(near_w[:units, :]))
    return total + dot(crossed_h[...], half(crossed_w[...])) + dot(far_h[...], half(far_w[...]))


def down_send_body(*refs):
    hidden, (down_ref, near_w, crossed_w, far_w, out_ref) = refs[:4], refs[4:]
    part = near_w.shape[1] // 2
    core = 1 - place_here() % 2
    total = down_sums(core, hidden, down_ref, near_w, crossed_w, far_w, part)
    out_ref[:, :part] = total.astype(BF)
    out_ref[:, part:] = jnp.zeros((total.shape[0], HALF), BF)


def down_keep_body(*refs):
    hidden, (down_ref, near_w, crossed_w, far_w, out_ref) = refs[:4], refs[4:]
    part = near_w.shape[1] // 2
    core = place_here() % 2
    out_ref[...] = down_sums(core, hidden, down_ref, near_w, crossed_w, far_w, part)


def repack_body(one_ref, two_ref, out_ref):
    rows, part = out_ref.shape[0], one_ref.shape[1]
    experts = rows // ROWS
    total = (one_ref[...] + two_ref[:, :part].astype(F32)).astype(BF)
    out_ref[:, :part] = total[:rows]
    repeat = (iota((rows, experts), 0) // ROWS == iota((rows, experts), 1)).astype(BF)
    out_ref[:, part:] = ninth_columns(dot(repeat, total[rows:]), part)


def combine_body(gates_ref, rows_ref, out_ref):
    steps, tokens, part = out_ref.shape
    values = rows_ref[...]
    total = dot(gates_ref[0], values) + dot(gates_ref[1], values)
    for step in range(steps):
        out = total[16 * step : 16 * step + tokens, :part]
        if step == steps - 1:
            more = [
                total[16 * (steps + i) : 16 * (steps + i) + tokens, part:]
                for i in range(part // HALF)
            ]
            out = out + jnp.concatenate(more, axis=1)
        out_ref[step] = out.astype(BF)


def local(
    latent_cache,
    new_latent,
    queries,
    lengths,
    token_rows,
    routes,
    route_gates,
    gate_proj,
    up_proj,
    down_proj,
):
    experts = lax.axis_size("grp")
    rows = experts * ROWS
    steps, tokens, width = token_rows.shape
    part = width // 8
    units = gate_proj.shape[2]
    down_proj = down_proj.reshape(units, width)
    packed, near_down, crossed_down = pl.pallas_call(
        pack_body,
        out_shape=[
            jax.ShapeDtypeStruct((rows, part + HALF), BF),
            jax.ShapeDtypeStruct((2 * units, 2 * part), BF),
            jax.ShapeDtypeStruct((units, 2 * part), BF),
        ],
        in_specs=[HBM] * 3,
        out_specs=[VMEM] * 3,
        scratch_shapes=[
            pltpu.VMEM((steps, tokens, 2 * part), BF),
            pltpu.VMEM((steps, routes.shape[2], tokens), jnp.int32),
            pltpu.VMEM((units, width), BF),
            pltpu.SemaphoreType.DMA((3,)),
        ],
        cost_estimate=pl.CostEstimate(flops=10**8, bytes_accessed=10**6, transcendentals=0),
        name="pack",
    )(token_rows, jnp.swapaxes(routes, 1, 2), down_proj)
    arrived = lax.all_to_all(
        packed.reshape(experts, ROWS, part + HALF), "grp", split_axis=0, concat_axis=0, tiled=True
    ).reshape(rows, part + HALF)

    gate_proj, up_proj = gate_proj.reshape(width, units), up_proj.reshape(width, units)
    near_down, crossed_down = to_near(near_down), to_crossed(crossed_down)
    arrived, near_down, crossed_down = lax.optimization_barrier(
        (arrived, near_down, crossed_down)
    )
    far_down = onward(near_down[units:])
    other = call(
        other_slices_body, jax.ShapeDtypeStruct((width // 2, 2 * units), BF),
        [VMEM] * 3, 10**6, 4 * 10**6, "other_slices",
    )(arrived, gate_proj, up_proj)
    other = swap(other, 1)

    pieces = gather(arrived)
    sums = jax.ShapeDtypeStruct((rows + experts, 2 * units), F32)
    send = call(
        partial_send_body, jax.ShapeDtypeStruct(sums.shape, BF), [VMEM] * 4 + [HBM, VMEM], 10**9, 4 * 10**6, "partial_send",
    )(*pieces, far_down, other)
    keep = call(
        partial_keep_body, sums, [VMEM] * 6, 10**9, 4 * 10**6, "partial_keep",
    )(*pieces, gate_proj, up_proj)
    hidden = call(
        hidden_body, jax.ShapeDtypeStruct((rows + experts, units), BF), [VMEM] * 2,
        10**7, 10**6, "hidden",
    )(keep, swap(send, 1))
    operands = *gather(hidden), down_proj, near_down, crossed_down, far_down
    send = call(
        down_send_body, jax.ShapeDtypeStruct((rows + experts, part + HALF), BF), [VMEM] * 8,
        10**9, 2 * 10**6, "down_send",
    )(*operands)
    keep = call(
        down_keep_body, jax.ShapeDtypeStruct((rows + experts, part), F32), [VMEM] * 8,
        10**9, 2 * 10**6, "down_keep",
    )(*operands)
    outgoing = call(
        repack_body, jax.ShapeDtypeStruct((rows, part + HALF), BF), [VMEM] * 2,
        10**8, 2 * 10**6, "repack",
    )(keep, swap(send, 1))
    returned = lax.all_to_all(
        outgoing.reshape(experts, ROWS, part + HALF), "grp", split_axis=0, concat_axis=0, tiled=True
    ).reshape(rows, part + HALF)

    heads = queries.shape[2]
    send, keep = call(
        attend_body, [jax.ShapeDtypeStruct((steps * heads, KL // 2 + 256), F32)] * 2,
        [HBM, SMEM, VMEM, VMEM, VMEM], 3 * 10**8, 2 * 10**6, "attend",
    )(
        outgoing,
        lengths,
        queries.reshape(steps * heads, queries.shape[3]),
        latent_cache[0].T,
        new_latent.reshape(steps, new_latent.shape[2]),
    )
    attention = call(
        merge_body, jax.ShapeDtypeStruct((steps * heads, KL // 2), BF), [VMEM, VMEM],
        10**6, 10**6, "merge",
    )(keep, swap(send, 4))
    gates = call(
        gates_body,
        jax.ShapeDtypeStruct((2, 16 * (steps + part // HALF), rows), BF),
        [HBM, VMEM, VMEM], 10**8, 10**6, "gates",
    )(outgoing, routes, route_gates)
    moe = call(
        combine_body, jax.ShapeDtypeStruct((steps, tokens, part), BF), [VMEM, VMEM],
        10**8, 10**6, "combine",
    )(gates, returned)
    return attention.reshape(steps, 1, heads, KL // 2), moe


def solution(mesh):
    in_specs = (
        P("grp", "sec", None),
        P(None, "grp", None),
        P(None, "grp", "tp", None),
        P("grp"),
        P(None, "grp", None),
        P(None, "grp", None),
        P(None, "grp", None),
        P("grp", None, ("sec", "tp")),
        P("grp", None, ("sec", "tp")),
        P("grp", ("sec", "tp"), None),
    )
    out_specs = (P(None, "grp", "tp", "sec"), P(None, "grp", ("sec", "tp")))
    return jax.shard_map(local, mesh=mesh, in_specs=in_specs, out_specs=out_specs, check_vma=False)
```
